32 devices in a mesh: expert: 8 (over z, y), grid: 4 (over x, core).
Axes of the slice: x: 2, y: 2, z: 4, core: 2. Of those that a mesh axis runs over, the one named last changes fastest.
Arguments:
- tokens: bfloat16 [4096, 1024], P(('expert', 'grid')), may hold values from -6 to 6
- routes: int32 [4096, 2], P(('expert', 'grid')), may hold values from 0 to 7, all different within a row; in each aligned block of 128 rows (0 to 127, 128 to 255, ...) at most 64 rows name the same one
- route_gates: float32 [4096, 2], P(('expert', 'grid')), may hold values from 0.2 to 1
- caption_lengths: int32 [32, 4], P(('expert', 'grid')), may hold values from 1 to 64, 128 in all within a row
- image_embed: bfloat16 [128, 1024], P(('expert', 'grid')), may hold values from -6 to 6
- final_gain: float32 [1024], replicated, may hold values from 0.1 to 1.9
- up_weight: bfloat16 [8, 1024, 4096], P('expert', None, 'grid'), may hold values from -0.1875 to 0.1875
- down_weight: bfloat16 [8, 1024, 4096], P('expert', None, 'grid'), may hold values from -0.09375 to 0.09375
Outputs:
- text_embed: float32 [128, 1024], P(('expert', 'grid'))
- sentence_direction_slope: float32 [128, 1024], P(('expert', 'grid'))
- picture_direction_slope: float32 [128, 1024], P(('expert', 'grid'))
The draws below stay inside these ranges and needn't reach their ends.
Inputs may be any that keep to these rules, and one draw needn't show every extreme that they name: `routes`: each token names two different experts; among the 128 tokens of one device no expert is named more than 64 times, and in every draw some device names some expert exactly 64 times. `caption_lengths`: each row gives the token counts of one device's 4 captions, summing to 128; the largest of a row is exactly 64.
All inputs are finite; a program needn't handle non-finite values.
Results may differ from the reference program's by a relative error of at most 0.003.
Values may be sent and summed in bfloat16 or wider, within the bound.
A program may use at most 64 MiB of HBM per device.

```python
import math
import jax
import jax.numpy as jnp
import numpy as np
from jax import lax

D = 1024
FF = 4096
TOK_DEV = 128
CAPT_DEV = 4
EXPERTS = 8
CAP = 64
TOKENS = 4096
CAPTIONS = 128
N_EXPERT = 8
N_GRID = 4


def shared_directions(key, owners):
    common = jax.random.normal(jax.random.fold_in(key, 101), (D,), jnp.float32)
    paired = jax.random.normal(jax.random.fold_in(key, 202), (owners, D), jnp.float32)
    owner_signs = jnp.where(jax.random.bernoulli(jax.random.fold_in(key, 303), 0.5, (owners,)), 1.0, -1.0).astype(jnp.float32)
    return (common, paired, owner_signs)


def draw_tokens(key, part):
    owners = TOKENS // TOK_DEV
    common, paired, owner_signs = shared_directions(key, owners)
    noise_key = jax.random.fold_in(key, 11)
    noise = jax.random.normal(noise_key, (owners, TOK_DEV, D), jnp.float32)
    common_amount = 0.1
    paired_amount = 0.2
    values = noise + common_amount * owner_signs[:, None, None] * common[None, None, :] + paired_amount * paired[:, None, :]
    return jnp.clip(values.reshape(TOKENS, D), -6.0, 6.0).astype(jnp.bfloat16)


def draw_image_embed(key, part):
    owners = TOKENS // TOK_DEV
    common, paired, owner_signs = shared_directions(key, owners)
    noise_key = jax.random.fold_in(key, 22)
    row_signs = jnp.where(jax.random.bernoulli(jax.random.fold_in(key, 404), 0.5, (CAPTIONS,)), 1.0, -1.0).astype(jnp.float32)
    noise = jax.random.normal(noise_key, (CAPTIONS, D), jnp.float32)
    strength = jax.random.uniform(jax.random.fold_in(key, 505), (CAPTIONS,), jnp.float32, 0.5, 1.5)
    common_amount = 0.3
    owner_rows = jnp.repeat(paired, CAPT_DEV, axis=0)
    values = noise + common_amount * row_signs[:, None] * common[None, :] + strength[:, None] * owner_rows
    return jnp.clip(values, -6.0, 6.0).astype(jnp.bfloat16)


def block_levels(stream_key, dims, shards, low, top_value):
    gain = 1.0
    for axis_at, shards_of in shards:
        draws = jax.random.uniform(jax.random.fold_in(jax.random.fold_in(stream_key, 6), axis_at), (shards_of,), jnp.float32, low / len(shards), top_value / len(shards))
        gain = gain * jnp.repeat(jnp.exp(draws), dims[axis_at] // shards_of).reshape((-1,) + (1,) * (len(dims) - 1 - axis_at))
    return gain


def split_up(count, total, most, skew):
    weights = [(1 << 20) // math.isqrt(standing ** skew) + 1 for standing in range(2, count + 1)]
    rest, holding = total - most - (count - 1), [1] * (count - 1)
    while rest > 0:
        candidates = [i for i in range(count - 1) if holding[i] < most]
        whole, left = sum([weights[i] for i in candidates]), rest
        for i in candidates:
            extra = min(most - holding[i], max(1, left * weights[i] // whole), rest)
            holding[i] = holding[i] + extra
            rest = rest - extra
    return np.array([most] + holding)


def uneven(key, count, total, most, skew):
    if count == 2:
        one = jax.random.randint(key, (), max(1, total - most), min(most, total - 1) + 1)
        return jnp.stack([one, total - one])
    lengths = jnp.asarray(split_up(count, total, most, skew), jnp.int32)
    twos = (count - 1) // 2
    giver, sink = lengths[1:1 + 2 * twos:2], lengths[2:2 + 2 * twos:2]
    margin = jnp.minimum(giver - 1, most - sink)
    moved = jax.random.randint(jax.random.fold_in(key, 1), (twos,), 0, 1 << 20) % (margin + 1)
    lengths = lengths.at[1:1 + 2 * twos:2].set(giver - moved).at[2:2 + 2 * twos:2].set(sink + moved)
    return lengths[jax.random.permutation(jax.random.fold_in(key, 2), count)]


def shared_out(own_key, own, number, rows, number_of, top, most, lean):
    order = jax.random.permutation(own_key, number_of)
    heavy_load, ordinary = shares(number_of, rows * top, most, lean, True), shares(number_of, rows * top, most, lean, False)
    places = jnp.arange(number_of)

    def named(sizes, turn):
        used = int((sizes > 0).sum())
        fixed = max(1, used // 4)
        moved = fixed + (places - fixed + turn * (used - fixed)) % max(1, number_of - fixed)
        return jnp.zeros((number_of,), jnp.int32).at[order[jnp.where(places < fixed, places, moved)]].set(jnp.asarray(sizes, jnp.int32))

    sizes = jnp.where(number % 4 == 0, named(heavy_load, number // 4), named(ordinary, number - number // 4 - 1))
    mixed = jax.random.permutation(jax.random.fold_in(own, 3), number_of)
    source_of, sink = mixed[0:number_of // 2 * 2:2], mixed[1:number_of // 2 * 2:2]
    margin = jnp.minimum(sizes[source_of] - 1, most - sizes[sink]) // 2
    margin = jnp.where((source_of == order[0]) | (sink == order[0]) | (sizes[sink] == 0), 0, jnp.maximum(margin, 0))
    moved = jax.random.randint(jax.random.fold_in(own, 4), (number_of // 2,), 0, 1 << 20) % (margin + 1)
    sizes = sizes.at[source_of].add(-moved).at[sink].add(moved)
    items = jnp.searchsorted(jnp.cumsum(sizes), jnp.arange(rows * top), side="right").astype(jnp.int32)
    table = items.reshape(top, rows).T
    table = table[jax.random.permutation(jax.random.fold_in(own, 1), rows)]
    turn = jax.random.randint(jax.random.fold_in(own, 2), (rows, 1), 0, top)
    return jnp.take_along_axis(table, (jnp.arange(top)[None, :] + turn) % top, axis=1)


def shares(number_of, total, most, slope, full):
    portions = [(1 << 20) // math.isqrt(grade ** slope) + 1 for grade in range(1, number_of + 1)]
    largest = most if full else min(most, max(-(-total // number_of), total * portions[0] // sum(portions)))
    least = 1 if total - largest >= number_of - 1 else 0
    given, spare = [largest] + [least] * (number_of - 1), total - largest - least * (number_of - 1)
    while spare > 0:
        movable = [i for i in range(1, number_of) if given[i] < largest] or [i for i in range(1, number_of) if given[i] < most]
        mass, left = sum([portions[i] for i in movable]), spare
        for i in movable:
            extra = min(most - given[i], max(1, left * portions[i] // mass), spare)
            given[i] = given[i] + extra
            spare = spare - extra
    return np.array(given)


def normal_values(rng, extent, width, most, split=(), held_as=jnp.bfloat16):
    entries = jax.random.normal(rng, extent, jnp.float32) * width
    if len(split) > 0:
        entries = block_levels(rng, extent, split, -0.22, 0.18) * entries
    return jnp.clip(entries, min=-most, max=most).astype(held_as)


def setup_inputs(seed: int = 0) -> dict:
    keys = jax.random.split(jax.random.key(seed), 9)
    tokens = draw_tokens(jax.random.fold_in(keys[8], 71), 0)
    routes_keys = jax.random.split(jax.random.fold_in(keys[1], 1), TOKENS // TOK_DEV)
    routes_turns = jax.random.permutation(jax.random.fold_in(keys[1], 3), TOKENS // TOK_DEV)
    routes = jax.vmap(lambda own, number: shared_out(jax.random.fold_in(keys[1], 2), own, number, TOK_DEV, EXPERTS, 2, CAP, 2))(routes_keys, routes_turns).reshape((TOKENS, 2))
    route_gates = jnp.clip(0.2 + 0.8 * jax.random.uniform(keys[2], (TOKENS, 2), jnp.float32) ** block_levels(keys[2], (TOKENS, 2), ((0, 32),), -0.2, 0.2), 0.2, 1.0)
    caption_lengths = jax.vmap(lambda own: uneven(own, CAPT_DEV, TOK_DEV, TOK_DEV // 2, 1))(jax.random.split(keys[3], (N_EXPERT * N_GRID))).reshape((N_EXPERT * N_GRID, CAPT_DEV)).astype(jnp.int32)
    image_embed = draw_image_embed(jax.random.fold_in(keys[8], 71), 0)
    final_gain = jnp.clip(1.0 + 0.18 * jax.random.normal(keys[5], (D,), jnp.float32), 0.1, 1.9)
    up_weight = normal_values(keys[6], (EXPERTS, D, FF), D ** -0.5, 0.1875, ((0, 8), (2, 4)))
    down_weight = normal_values(keys[7], (EXPERTS, D, FF), FF ** -0.5, 0.09375, ((0, 8), (2, 4)))
    return dict(tokens=tokens, routes=routes, route_gates=route_gates, caption_lengths=caption_lengths, image_embed=image_embed, final_gain=final_gain, up_weight=up_weight, down_weight=down_weight)


EPSILON = 1e-06
SIMILARITY_HEAT = 10.0

def layer_norm(values):
    centred = values - lax.optimization_barrier(jnp.mean(values, axis=-1, keepdims=True))
    return centred * lax.rsqrt(lax.optimization_barrier(jnp.mean(centred * centred, axis=-1, keepdims=True)) + EPSILON)

def reference(tokens, routes, route_gates, caption_lengths, image_embed, final_gain, up_weight, down_weight):
    devices = N_EXPERT * N_GRID
    stream = tokens.astype(jnp.float32).reshape(devices, TOK_DEV, D)
    normed = layer_norm(stream).astype(jnp.bfloat16)
    chosen = routes.reshape(devices, 2 * TOK_DEV)
    expert_hot = (chosen[:, :, None] == jnp.arange(EXPERTS, dtype=jnp.int32)[None, None, :]).astype(jnp.int32)
    before = jnp.cumsum(expert_hot, axis=1) - expert_hot
    slot_of = lax.optimization_barrier(jnp.sum(before * expert_hot, axis=2)).astype(jnp.int32)
    position = (chosen * CAP + slot_of).astype(jnp.int32)

    def build(inputs):
        rows, places = inputs
        repeated = jnp.repeat(rows, 2, axis=0)
        return jnp.zeros((EXPERTS * CAP, D), jnp.bfloat16).at[places].set(repeated)
    buffers = lax.map(build, (normed, position))
    per_expert = buffers.reshape(devices, EXPERTS, CAP, D).transpose(1, 0, 2, 3).reshape(EXPERTS, devices * CAP, D)
    quarter = FF // N_GRID

    def run_expert(inputs):
        rows, up_matrix, down_matrix = inputs
        total = jnp.zeros((rows.shape[0], D), jnp.float32)
        for index in range(N_GRID):
            low = index * quarter
            hidden = jax.nn.gelu(jnp.dot(rows, up_matrix[:, low:low + quarter], preferred_element_type=jnp.float32), approximate=False).astype(jnp.bfloat16)
            term = jnp.dot(hidden, down_matrix[:, low:low + quarter].T, preferred_element_type=jnp.float32)
            total = total + lax.optimization_barrier(term.astype(jnp.bfloat16)).astype(jnp.float32)
        return total.astype(jnp.bfloat16)
    outputs = lax.map(run_expert, (per_expert, up_weight, down_weight))
    back = outputs.reshape(EXPERTS, devices, CAP, D).transpose(1, 0, 2, 3).reshape(devices, EXPERTS * CAP, D)
    picked = jax.vmap(lambda table, places: table[places])(back, position).astype(jnp.float32)
    weighted = picked * route_gates.reshape(devices, 2 * TOK_DEV)[:, :, None]
    mixed = stream + lax.optimization_barrier(jnp.sum(weighted.reshape(devices, TOK_DEV, 2, D), axis=2))
    final = layer_norm(mixed) * final_gain
    ends = jnp.cumsum(caption_lengths, axis=1)
    starts = ends - caption_lengths
    spots = jnp.arange(TOK_DEV, dtype=jnp.int32)
    members = ((spots[None, None, :] >= starts[:, :, None]) & (spots[None, None, :] < ends[:, :, None])).astype(jnp.float32)
    pooled = jnp.einsum('sct,std->scd', members, final, precision=lax.Precision.HIGHEST)
    pooled = pooled / caption_lengths[:, :, None].astype(jnp.float32)
    pooled = pooled.reshape(CAPTIONS, D)
    text_embed = pooled * lax.rsqrt(lax.optimization_barrier(jnp.mean(pooled * pooled, axis=-1, keepdims=True)) + EPSILON)
    root = jnp.sqrt(jnp.float32(D))
    sentence_average = (text_embed / root).astype(jnp.bfloat16)
    sentence_direction = sentence_average.astype(jnp.float32)
    image_values = image_embed.astype(jnp.float32)
    picture_average = (image_values * lax.rsqrt(lax.optimization_barrier(jnp.mean(image_values * image_values, axis=-1, keepdims=True)) + EPSILON) / root).astype(jnp.bfloat16)
    picture_direction = picture_average.astype(jnp.float32)
    match_similarity_matrix = SIMILARITY_HEAT * jnp.dot(picture_average, sentence_average.T, preferred_element_type=jnp.float32)
    labels = jnp.arange(CAPTIONS, dtype=jnp.int32)
    signs = jnp.where(labels[:, None] == labels[None, :], 1.0, -1.0).astype(jnp.float32)
    objective_multiplier = -signs * jax.nn.sigmoid(-signs * match_similarity_matrix)
    picture_direction_slope = SIMILARITY_HEAT * jnp.dot(objective_multiplier, sentence_direction, precision=lax.Precision.HIGHEST)
    sentence_direction_slope = SIMILARITY_HEAT * jnp.dot(objective_multiplier.T, picture_direction, precision=lax.Precision.HIGHEST)
    return (text_embed, sentence_direction_slope, picture_direction_slope)
```

```python
import functools
import math

import jax
import jax.numpy as jnp
from jax import lax
from jax.experimental import pallas as pl
from jax.experimental.pallas import tpu as pltpu
from jax.sharding import PartitionSpec as P

EPSILON = 1e-06
SIMILARITY_HEAT = 10.0
MESH = pl.DeviceIdType.MESH
BF16 = jnp.bfloat16
F32 = jnp.float32


def layer_norm(values):
    centred = values - jnp.mean(values, axis=-1, keepdims=True)
    return centred * lax.rsqrt(jnp.mean(centred * centred, axis=-1, keepdims=True) + EPSILON)


def root_norm(values):
    return values * lax.rsqrt(jnp.mean(values * values, axis=-1, keepdims=True) + EPSILON)


def flip(one, other, count):
    total, bit = 0, 1
    while bit < count:
        total = total + bit * (((one // bit) + (other // bit)) % 2)
        bit *= 2
    return total


def halves(values):
    high = values.astype(BF16)
    return high, (values - high.astype(F32)).astype(BF16)


def dot(left, right):
    return jnp.dot(left, right, preferred_element_type=F32)


def dot_nt(left, right):
    return lax.dot_general(left, right, (((1,), (1,)), ((), ())), preferred_element_type=F32)


def join(values, rows):
    width = values.shape[-1]
    if values.shape[-2] % 16 == 0:
        return values.reshape(rows, width)
    return values.astype(F32).reshape(rows, width).astype(values.dtype)


def part(values, lead):
    return values.reshape(lead + (values.shape[0] // math.prod(lead), values.shape[-1]))


def slope(own, every, offset):
    logits = SIMILARITY_HEAT * dot_nt(own, every)
    row = lax.broadcasted_iota(jnp.int32, logits.shape, 0)
    column = lax.broadcasted_iota(jnp.int32, logits.shape, 1)
    signs = jnp.where(column == row + offset, 1.0, -1.0).astype(F32)
    coeff = -signs * jax.nn.sigmoid(-signs * logits)
    high, low = halves(coeff)
    return SIMILARITY_HEAT * (dot(high, every) + dot(low, every))


def kernel(
    experts, grids, slots, captions,
    lengths_ref, tokens_ref, routes_ref, gates_ref, image_ref, gain_ref, up_hbm, down_hbm,
    embed_ref, sentence_ref, picture_ref,
    up_ref, down_ref, send, gate_high, gate_low, rows, own, part_send, part_in, sum_send, sum_in,
    back_send, back_in, own_image, near_image, all_image, own_text, near_text, all_text,
    weight_sem, to_expert_s, to_expert_r, fx_s, fx_r, fc_s, fc_r, part_s, part_r, sum_s, sum_r,
    back_s, back_r, near_s, near_r, far_s, far_r,
):
    e = lax.axis_index("expert")
    g = lax.axis_index("grid")
    core = (e, g + 1 - 2 * (g % 2))
    cross = (e, (g + grids // 2) % grids)
    tokens, width = tokens_ref.shape
    group = grids * captions

    def expert_peer(step):
        return (flip(e, step, experts), g)

    def push(source, target, send_sem, recv_sem, device):
        pltpu.make_async_remote_copy(
            src_ref=source, dst_ref=target, send_sem=send_sem, recv_sem=recv_sem,
            device_id=device, device_id_type=MESH,
        ).start()

    def await_bytes(ref, sem):
        pltpu.make_async_copy(ref, ref, sem).wait()

    barrier = pltpu.get_barrier_semaphore()

    def greet(step, carry):
        pl.semaphore_signal(barrier, inc=1, device_id=expert_peer(step), device_id_type=MESH)
        return carry

    lax.fori_loop(1, experts, greet, 0)
    for hop in range(1, grids):
        pl.semaphore_signal(barrier, inc=1, device_id=(e, (g + hop) % grids), device_id_type=MESH)
    load_up = pltpu.make_async_copy(up_hbm, up_ref, weight_sem.at[0])
    load_up.start()
    load_down = pltpu.make_async_copy(down_hbm, down_ref, weight_sem.at[1])
    load_down.start()

    normed = layer_norm(tokens_ref[...].astype(F32)).astype(BF16)
    routes = routes_ref[...]
    first, second = routes[0:1, :], routes[1:2, :]
    ids = lax.broadcasted_iota(jnp.int32, (max(experts, 8), tokens), 0)
    named = ((ids == first) | (ids == second)).astype(F32).astype(BF16)
    before = lax.broadcasted_iota(jnp.int32, (tokens, tokens), 0)
    after = lax.broadcasted_iota(jnp.int32, (tokens, tokens), 1)
    ranks = dot(named, (before < after).astype(F32).astype(BF16))
    spots = lax.broadcasted_iota(jnp.int32, (experts * slots, tokens), 0)
    taken = None
    weights = None
    for choice, chosen in enumerate((first, second)):
        rank = jnp.sum(jnp.where(ids == chosen, ranks, 0.0), axis=0, keepdims=True)
        place = flip(chosen, e, experts) * slots + rank.astype(jnp.int32)
        hit = spots == place
        weight = jnp.where(hit, gates_ref[choice:choice + 1, :], 0.0)
        taken = hit if taken is None else taken | hit
        weights = weight if weights is None else weights + weight
    blocks = part(dot(taken.astype(F32).astype(BF16), normed), (experts,)).astype(BF16)
    send[...] = blocks
    rows[0, 0] = blocks[0]
    high, low = halves(weights.T)
    gate_high[...] = high
    gate_low[...] = low

    line = lax.broadcasted_iota(jnp.int32, (2 * group, 1), 0)
    caption = jnp.where(line < group, line - g * captions, line - group)
    images = root_norm(image_ref[...].astype(F32)) / math.sqrt(width)
    spread = jnp.zeros((2 * group, width), F32)
    for index in range(captions):
        spread = jnp.where(caption == index, images[index:index + 1, :], spread)
    near_image[0] = spread[:group].astype(BF16)
    own_image[...] = spread[group:].astype(BF16)

    pl.semaphore_wait(barrier, experts + grids - 2)

    def dispatch(step, carry):
        push(send.at[step], rows.at[step, 0], to_expert_s, to_expert_r.at[step], expert_peer(step))
        return carry

    lax.fori_loop(1, experts, dispatch, 0)

    def share_near(near, index):
        for hop in range(1, grids):
            push(near.at[0], near.at[hop], near_s.at[index], near_r.at[index], (e, (g + hop) % grids))

    def share_far(near, every, index):
        await_bytes(near.at[pl.ds(1, grids - 1)], near_r.at[index])
        total = near[0].astype(F32)
        for hop in range(1, grids):
            total = total + near[hop].astype(F32)
        every[0] = total.astype(BF16)

        def each(step, carry):
            push(every.at[0], every.at[step], far_s.at[index], far_r.at[index], expert_peer(step))
            return carry

        lax.fori_loop(1, experts, each, 0)

    share_near(near_image, 0)

    def turn(index, carry):
        @pl.when(index < experts)
        def _():
            at = index

            @pl.when(at > 0)
            def _():
                await_bytes(rows.at[at, 0], to_expert_r.at[at])

            push(rows.at[at, 0], rows.at[at, 1], fx_s, fx_r.at[at], cross)
            push(rows.at[at, 0], rows.at[at, 2], fc_s, fc_r.at[at], core)

        @pl.when((index >= 1) & (index < experts + 1))
        def _():
            at = index - 1
            await_bytes(rows.at[at, 1], fx_r.at[at])
            push(rows.at[at, 1], rows.at[at, 3], fc_s, fc_r.at[at], core)

        @pl.when(index == 1)
        def _():
            share_far(near_image, all_image, 0)
            load_up.wait()
            load_down.wait()

        @pl.when((index >= 2) & (index < experts + 2))
        def _():
            at = index - 2
            await_bytes(rows.at[at, pl.ds(2, 2)], fc_r.at[at])
            block = join(rows[at], grids * slots)
            inner = dot(block, up_ref[...])
            hidden = (0.5 * inner * (1.0 + lax.erf(inner * math.sqrt(0.5)))).astype(BF16)
            term = part(dot_nt(hidden, down_ref[...]), (grids,))
            own[at] = term[:2]
            part_send[at] = term[2:].astype(BF16)
            push(part_send.at[at], part_in.at[at], part_s, part_r.at[at], core)

        @pl.when((index >= 3) & (index < experts + 3))
        def _():
            at = index - 3
            await_bytes(part_in.at[at], part_r.at[at])
            sum_send[at] = (own[at, 1] + part_in[at, 1].astype(F32)).astype(BF16)
            push(sum_send.at[at], sum_in.at[at], sum_s, sum_r.at[at], cross)

        @pl.when(index >= 4)
        def _():
            at = index - 4
            await_bytes(sum_in.at[at], sum_r.at[at])
            result = own[at, 0] + part_in[at, 0].astype(F32) + sum_in[at].astype(F32)

            @pl.when(at == 0)
            def _():
                back_in[0] = result.astype(BF16)

            @pl.when(at > 0)
            def _():
                back_send[at] = result.astype(BF16)
                push(back_send.at[at], back_in.at[at], back_s, back_r, expert_peer(at))

        return carry

    lax.fori_loop(0, experts + 4, turn, 0)

    await_bytes(back_in.at[pl.ds(1, experts - 1)], back_r)
    returned = join(back_in[...], experts * slots)
    picked = dot(gate_high[...], returned) + dot(gate_low[...], returned)
    final = layer_norm(tokens_ref[...].astype(F32) + picked) * gain_ref[...]
    starts = jnp.zeros((2 * group, 1), jnp.int32)
    ends = jnp.zeros((2 * group, 1), jnp.int32)
    reached = 0
    for index in range(captions):
        starts = jnp.where(caption == index, reached, starts)
        reached = reached + lengths_ref[0, index]
        ends = jnp.where(caption == index, reached, ends)
    spot = lax.broadcasted_iota(jnp.int32, (2 * group, tokens), 1)
    members = ((spot >= starts) & (spot < ends)).astype(F32).astype(BF16)
    high, low = halves(final)
    pooled = (dot(members, high) + dot(members, low)) / jnp.maximum(ends - starts, 1).astype(F32)
    embed = root_norm(pooled)
    embed_ref[...] = embed[group:group + captions]
    direction = embed / math.sqrt(width)
    near_text[0] = direction[:group].astype(BF16)
    own_text[...] = direction[group:].astype(BF16)
    share_near(near_text, 1)
    share_far(near_text, all_text, 1)

    others = pl.ds(1, experts - 1)
    await_bytes(all_image.at[others], far_r.at[0])
    images_all = all_image[...].reshape(experts * group, width)
    offset = g * captions
    sentence_ref[...] = slope(own_text[...], images_all, offset)[:captions]
    await_bytes(all_text.at[others], far_r.at[1])
    texts_all = all_text[...].reshape(experts * group, width)
    picture_ref[...] = slope(own_image[...], texts_all, offset)[:captions]

    await_bytes(send.at[others], to_expert_s)
    await_bytes(send, fx_s)
    await_bytes(part_send, fc_s)
    await_bytes(part_send, part_s)
    await_bytes(sum_send, sum_s)
    await_bytes(back_send.at[others], back_s)
    for index, (near, every) in enumerate(((near_image, all_image), (near_text, all_text))):
        await_bytes(near.at[pl.ds(1, grids - 1)], near_s.at[index])
        await_bytes(every.at[others], far_s.at[index])


def on_device(
    tokens, routes, route_gates, caption_lengths, image_embed, final_gain, up_weight, down_weight
):
    count, width = tokens.shape
    experts, grids = lax.axis_size("expert"), lax.axis_size("grid")
    slots = 4 * count // experts
    captions = caption_lengths.shape[1]
    group = grids * captions
    inner = up_weight.shape[2]
    dma = pltpu.SemaphoreType.DMA
    whole = pl.BlockSpec(memory_space=pltpu.VMEM)
    far = pl.BlockSpec(memory_space=pl.ANY)
    out = jax.ShapeDtypeStruct((captions, width), F32)
    scratch = [
        pltpu.VMEM((width, inner), BF16),
        pltpu.VMEM((width, inner), BF16),
        pltpu.VMEM((experts, slots, width), BF16),
        pltpu.VMEM((count, experts * slots), BF16),
        pltpu.VMEM((count, experts * slots), BF16),
        pltpu.VMEM((experts, grids, slots, width), BF16),
        pltpu.VMEM((experts, 2, slots, width), F32),
        pltpu.VMEM((experts, 2, slots, width), BF16),
        pltpu.VMEM((experts, 2, slots, width), BF16),
    ] + [pltpu.VMEM((experts, slots, width), BF16)] * 4 + [
        pltpu.VMEM((group, width), BF16),
        pltpu.VMEM((grids, group, width), BF16),
        pltpu.VMEM((experts, group, width), BF16),
    ] * 2 + [
        dma((2,)),
        dma, dma((experts,)),
        dma, dma((experts,)),
        dma, dma((experts,)),
        dma, dma((experts,)),
        dma, dma((experts,)),
        dma, dma,
        dma((2,)), dma((2,)), dma((2,)), dma((2,)),
    ]
    rows = experts * slots * grids
    return pl.pallas_call(
        functools.partial(kernel, experts, grids, slots, captions),
        out_shape=(out, out, out),
        in_specs=[pl.BlockSpec(memory_space=pltpu.SMEM)] + [whole] * 5 + [far] * 2,
        out_specs=(whole, whole, whole),
        scratch_shapes=scratch,
        cost_estimate=pl.CostEstimate(
            flops=4 * rows * width * inner, bytes_accessed=4 * width * inner,
            transcendentals=rows * inner,
        ),
        compiler_params=pltpu.CompilerParams(
            collective_id=0, has_side_effects=True, vmem_limit_bytes=56 * 1024 * 1024
        ),
    )(
        caption_lengths, tokens, routes.T, route_gates.T, image_embed, final_gain[None, :],
        up_weight[0], down_weight[0],
    )


def solution(mesh):
    split = P(("expert", "grid"), None)
    return jax.shard_map(
        on_device,
        mesh=mesh,
        in_specs=(split,) * 5 + (P(), P("expert", None, "grid"), P("expert", None, "grid")),
        out_specs=(split,) * 3,
        check_vma=False,
    )
```

```python
import functools
import math

import jax
import jax.numpy as jnp
from jax import lax
from jax.experimental import pallas as pl
from jax.experimental.pallas import tpu as pltpu
from jax.sharding import PartitionSpec as P

EPSILON = 1e-06
SIMILARITY_HEAT = 10.0
MESH = pl.DeviceIdType.MESH
BF16 = jnp.bfloat16
F32 = jnp.float32


def layer_norm(values):
    centred = values - jnp.mean(values, axis=-1, keepdims=True)
    return centred * lax.rsqrt(jnp.mean(centred * centred, axis=-1, keepdims=True) + EPSILON)


def root_norm(values):
    return values * lax.rsqrt(jnp.mean(values * values, axis=-1, keepdims=True) + EPSILON)


def flip(one, other, count):
    total, bit = 0, 1
    while bit < count:
        total = total + bit * (((one // bit) + (other // bit)) % 2)
        bit *= 2
    return total


def halves(values):
    high = values.astype(BF16)
    return high, (values - high.astype(F32)).astype(BF16)


def dot(left, right):
    return jnp.dot(left, right, preferred_element_type=F32)


def dot_nt(left, right):
    return lax.dot_general(left, right, (((1,), (1,)), ((), ())), preferred_element_type=F32)


def join(values, rows):
    width = values.shape[-1]
    if values.shape[-2] % 16 == 0:
        return values.reshape(rows, width)
    return values.astype(F32).reshape(rows, width).astype(values.dtype)


def part(values, lead):
    return values.reshape(lead + (values.shape[0] // math.prod(lead), values.shape[-1]))


def slope(own, every, offset):
    logits = SIMILARITY_HEAT * dot_nt(own, every)
    row = lax.broadcasted_iota(jnp.int32, logits.shape, 0)
    column = lax.broadcasted_iota(jnp.int32, logits.shape, 1)
    signs = jnp.where(column == row + offset, 1.0, -1.0).astype(F32)
    coeff = -signs * jax.nn.sigmoid(-signs * logits)
    high, low = halves(coeff)
    return SIMILARITY_HEAT * (dot(high, every) + dot(low, every))


def kernel(
    experts, grids, slots, captions,
    lengths_ref, tokens_ref, meta_ref, image_ref, gain_ref, up_hbm, down_hbm,
    embed_ref, sentence_ref, picture_ref,
    up_ref, down_ref, normed, relay_rows, relay_meta, relay_sum, far_sum,
    send, gate_high, gate_low, rows, own, part_send, part_in, sum_send, sum_in,
    back_send, back_in, own_image, near_image, all_image, own_text, near_text, all_text,
    weight_sem, relay_s, relay_r, to_expert_s, to_expert_r, fx_s, fx_r, fc_s, fc_r, part_s, part_r, sum_s, sum_r,
    back_s, back_r, near_s, near_r, far_s, far_r,
):
    e = lax.axis_index("expert")
    g = lax.axis_index("grid")
    core = (e, g + 1 - 2 * (g % 2))
    cross = (e, (g + grids // 2) % grids)
    tokens, width = tokens_ref.shape
    group = grids * captions
    half = experts // 2
    early = half // 2
    opposite = ((e + half) % experts, g)

    def expert_peer(step):
        return (flip(e, step, experts), g)

    def near_peer(step):
        return (flip(e, step % half, experts), g)

    def push(source, target, send_sem, recv_sem, device):
        pltpu.make_async_remote_copy(
            src_ref=source, dst_ref=target, send_sem=send_sem, recv_sem=recv_sem,
            device_id=device, device_id_type=MESH,
        ).start()

    def await_bytes(ref, sem):
        pltpu.make_async_copy(ref, ref, sem).wait()

    barrier = pltpu.get_barrier_semaphore()

    def greet(step, carry):
        pl.semaphore_signal(barrier, inc=1, device_id=expert_peer(step), device_id_type=MESH)
        return carry

    lax.fori_loop(1, experts, greet, 0)
    for hop in range(1, grids):
        pl.semaphore_signal(barrier, inc=1, device_id=(e, (g + hop) % grids), device_id_type=MESH)
    load_up = pltpu.make_async_copy(up_hbm, up_ref, weight_sem.at[0])
    load_up.start()
    load_down = pltpu.make_async_copy(down_hbm, down_ref, weight_sem.at[1])
    load_down.start()

    normed[...] = layer_norm(tokens_ref[...].astype(F32)).astype(BF16)
    pl.semaphore_wait(barrier, experts + grids - 2)
    push(normed, relay_rows, relay_s.at[0], relay_r.at[0], opposite)
    push(meta_ref, relay_meta, relay_s.at[1], relay_r.at[1], opposite)

    def place_rows(values, meta, which):
        routes = meta[0:2, :].astype(jnp.int32)
        gates = meta[2:4, :]
        first, second = routes[0:1, :], routes[1:2, :]
        ids = lax.broadcasted_iota(jnp.int32, (max(experts, 8), tokens), 0)
        named = ((ids == first) | (ids == second)).astype(F32).astype(BF16)
        before = lax.broadcasted_iota(jnp.int32, (tokens, tokens), 0)
        after = lax.broadcasted_iota(jnp.int32, (tokens, tokens), 1)
        ranks = dot(named, (before < after).astype(F32).astype(BF16))
        spots = lax.broadcasted_iota(jnp.int32, (half * slots, tokens), 0)
        taken = None
        weights = None
        for choice, chosen in enumerate((first, second)):
            rank = jnp.sum(jnp.where(ids == chosen, ranks, 0.0), axis=0, keepdims=True)
            hit = spots == flip(chosen, e, experts) * slots + rank.astype(jnp.int32)
            weight = jnp.where(hit, gates[choice:choice + 1, :], 0.0)
            taken = hit if taken is None else taken | hit
            weights = weight if weights is None else weights + weight
        blocks = part(dot(taken.astype(F32).astype(BF16), values), (half,)).astype(BF16)
        gate_high[which], gate_low[which] = halves(weights.T)
        return blocks

    blocks = place_rows(normed[...], meta_ref[...], 0)
    send[:early] = blocks[:early]
    send[half + early:] = blocks[early:]
    rows[0, 0] = blocks[0]

    def dispatch(step, carry):
        push(send.at[step], rows.at[step, 0], to_expert_s, to_expert_r.at[step], near_peer(step))
        return carry

    lax.fori_loop(1, early, dispatch, 0)
    lax.fori_loop(half + early, experts, dispatch, 0)

    line = lax.broadcasted_iota(jnp.int32, (2 * group, 1), 0)
    caption = jnp.where(line < group, line - g * captions, line - group)
    images = root_norm(image_ref[...].astype(F32)) / math.sqrt(width)
    spread = jnp.zeros((2 * group, width), F32)
    for index in range(captions):
        spread = jnp.where(caption == index, images[index:index + 1, :], spread)
    near_image[0] = spread[:group].astype(BF16)
    own_image[...] = spread[group:].astype(BF16)

    def share_near(near, index):
        for hop in range(1, grids):
            push(near.at[0], near.at[hop], near_s.at[index], near_r.at[index], (e, (g + hop) % grids))

    def share_far(near, every, index):
        await_bytes(near.at[pl.ds(1, grids - 1)], near_r.at[index])
        total = near[0].astype(F32)
        for hop in range(1, grids):
            total = total + near[hop].astype(F32)
        every[0] = total.astype(BF16)

        def each(step, carry):
            push(every.at[0], every.at[step], far_s.at[index], far_r.at[index], expert_peer(step))
            return carry

        lax.fori_loop(1, experts, each, 0)

    share_near(near_image, 0)

    def await_back(low, high):
        def each(step, carry):
            await_bytes(back_in.at[step], back_r.at[step])
            return carry

        lax.fori_loop(low, high, each, 0)

    def combine(which, one, other):
        cut = one.shape[0]
        total = dot(gate_high[which, :, :cut], one) + dot(gate_low[which, :, :cut], one)
        return total + dot(gate_high[which, :, cut:], other) + dot(gate_low[which, :, cut:], other)

    def turn(index, carry):
        @pl.when(index < experts)
        def _():
            at = index

            @pl.when(at % half > 0)
            def _():
                await_bytes(rows.at[at, 0], to_expert_r.at[at])

            push(rows.at[at, 0], rows.at[at, 1], fx_s, fx_r.at[at], cross)
            push(rows.at[at, 0], rows.at[at, 2], fc_s, fc_r.at[at], core)

        @pl.when((index >= 1) & (index < experts + 1))
        def _():
            at = index - 1
            await_bytes(rows.at[at, 1], fx_r.at[at])
            push(rows.at[at, 1], rows.at[at, 3], fc_s, fc_r.at[at], core)

        @pl.when(index == 1)
        def _():
            await_bytes(relay_rows, relay_r.at[0])
            await_bytes(relay_meta, relay_r.at[1])
            blocks = place_rows(relay_rows[...], relay_meta[...], 1)
            send[early:half] = blocks[early:]
            send[half:half + early] = blocks[:early]
            rows[half, 0] = blocks[0]
            lax.fori_loop(early, half, dispatch, 0)
            lax.fori_loop(half + 1, half + early, dispatch, 0)
            share_far(near_image, all_image, 0)
            load_up.wait()
            load_down.wait()

        @pl.when((index >= 2) & (index < experts + 2))
        def _():
            at = index - 2
            await_bytes(rows.at[at, pl.ds(2, 2)], fc_r.at[at])
            block = join(rows[at], grids * slots)
            inner = dot(block, up_ref[...])
            hidden = (0.5 * inner * (1.0 + lax.erf(inner * math.sqrt(0.5)))).astype(BF16)
            term = part(dot_nt(hidden, down_ref[...]), (grids,))
            own[at] = term[:2]
            part_send[at] = term[2:].astype(BF16)
            push(part_send.at[at], part_in.at[at], part_s, part_r.at[at], core)

        @pl.when((index >= 3) & (index < experts + 3))
        def _():
            at = index - 3
            await_bytes(part_in.at[at], part_r.at[at])
            sum_send[at] = (own[at, 1] + part_in[at, 1].astype(F32)).astype(BF16)
            push(sum_send.at[at], sum_in.at[at], sum_s, sum_r.at[at], cross)

        @pl.when(index == experts + 3)
        def _():
            await_back(early, half)
            await_back(half + 1, half + early)
            relay_sum[...] = combine(
                1, join(back_in[half:half + early], early * slots),
                join(back_in[early:half], (half - early) * slots),
            ).astype(BF16)
            push(relay_sum, far_sum, relay_s.at[2], relay_r.at[2], opposite)

        @pl.when(index >= 4)
        def _():
            at = index - 4
            await_bytes(sum_in.at[at], sum_r.at[at])
            result = own[at, 0] + part_in[at, 0].astype(F32) + sum_in[at].astype(F32)

            @pl.when(at % half == 0)
            def _():
                back_in[at] = result.astype(BF16)

            @pl.when(at % half > 0)
            def _():
                back_send[at] = result.astype(BF16)
                push(back_send.at[at], back_in.at[at], back_s, back_r.at[at], near_peer(at))

        return carry

    lax.fori_loop(0, experts + 4, turn, 0)

    await_back(1, early)
    await_back(half + early, experts)
    picked = combine(
        0, join(back_in[:early], early * slots),
        join(back_in[half + early:], (half - early) * slots),
    )
    await_bytes(far_sum, relay_r.at[2])
    picked = picked + far_sum[...].astype(F32)
    final = layer_norm(tokens_ref[...].astype(F32) + picked) * gain_ref[...]
    starts = jnp.zeros((2 * group, 1), jnp.int32)
    ends = jnp.zeros((2 * group, 1), jnp.int32)
    reached = 0
    for index in range(captions):
        starts = jnp.where(caption == index, reached, starts)
        reached = reached + lengths_ref[0, index]
        ends = jnp.where(caption == index, reached, ends)
    spot = lax.broadcasted_iota(jnp.int32, (2 * group, tokens), 1)
    members = ((spot >= starts) & (spot < ends)).astype(F32).astype(BF16)
    high, low = halves(final)
    pooled = (dot(members, high) + dot(members, low)) / jnp.maximum(ends - starts, 1).astype(F32)
    embed = root_norm(pooled)
    embed_ref[...] = embed[group:group + captions]
    direction = embed / math.sqrt(width)
    near_text[0] = direction[:group].astype(BF16)
    own_text[...] = direction[group:].astype(BF16)
    share_near(near_text, 1)
    share_far(near_text, all_text, 1)

    others = pl.ds(1, experts - 1)
    await_bytes(all_image.at[others], far_r.at[0])
    images_all = all_image[...].reshape(experts * group, width)
    offset = g * captions
    sentence_ref[...] = slope(own_text[...], images_all, offset)[:captions]
    await_bytes(all_text.at[others], far_r.at[1])
    texts_all = all_text[...].reshape(experts * group, width)
    picture_ref[...] = slope(own_image[...], texts_all, offset)[:captions]

    await_bytes(normed, relay_s.at[0])
    await_bytes(meta_ref, relay_s.at[1])
    await_bytes(relay_sum, relay_s.at[2])
    apart = pl.ds(1, experts - 2)
    await_bytes(send.at[apart], to_expert_s)
    await_bytes(send, fx_s)
    await_bytes(part_send, fc_s)
    await_bytes(part_send, part_s)
    await_bytes(sum_send, sum_s)
    await_bytes(back_send.at[apart], back_s)
    for index, (near, every) in enumerate(((near_image, all_image), (near_text, all_text))):
        await_bytes(near.at[pl.ds(1, grids - 1)], near_s.at[index])
        await_bytes(every.at[others], far_s.at[index])


def on_device(
    tokens, routes, route_gates, caption_lengths, image_embed, final_gain, up_weight, down_weight
):
    count, width = tokens.shape
    experts, grids = lax.axis_size("expert"), lax.axis_size("grid")
    slots = 4 * count // experts
    captions = caption_lengths.shape[1]
    group = grids * captions
    inner = up_weight.shape[2]
    dma = pltpu.SemaphoreType.DMA
    whole = pl.BlockSpec(memory_space=pltpu.VMEM)
    far = pl.BlockSpec(memory_space=pl.ANY)
    out = jax.ShapeDtypeStruct((captions, width), F32)
    scratch = [
        pltpu.VMEM((width, inner), BF16),
        pltpu.VMEM((width, inner), BF16),
        pltpu.VMEM((count, width), BF16),
        pltpu.VMEM((count, width), BF16),
        pltpu.VMEM((8, count), F32),
        pltpu.VMEM((count, width), BF16),
        pltpu.VMEM((count, width), BF16),
        pltpu.VMEM((experts, slots, width), BF16),
        pltpu.VMEM((2, count, experts * slots // 2), BF16),
        pltpu.VMEM((2, count, experts * slots // 2), BF16),
        pltpu.VMEM((experts, grids, slots, width), BF16),
        pltpu.VMEM((experts, 2, slots, width), F32),
        pltpu.VMEM((experts, 2, slots, width), BF16),
        pltpu.VMEM((experts, 2, slots, width), BF16),
    ] + [pltpu.VMEM((experts, slots, width), BF16)] * 4 + [
        pltpu.VMEM((group, width), BF16),
        pltpu.VMEM((grids, group, width), BF16),
        pltpu.VMEM((experts, group, width), BF16),
    ] * 2 + [
        dma((2,)), dma((3,)), dma((3,)),
        dma, dma((experts,)),
        dma, dma((experts,)),
        dma, dma((experts,)),
        dma, dma((experts,)),
        dma, dma((experts,)),
        dma, dma((experts,)),
        dma((2,)), dma((2,)), dma((2,)), dma((2,)),
    ]
    rows = experts * slots * grids
    meta = jnp.concatenate([routes.astype(F32), route_gates], axis=1).T
    meta = jnp.pad(meta, ((0, 8 - meta.shape[0]), (0, 0)))
    return pl.pallas_call(
        functools.partial(kernel, experts, grids, slots, captions),
        out_shape=(out, out, out),
        in_specs=[pl.BlockSpec(memory_space=pltpu.SMEM)] + [whole] * 4 + [far] * 2,
        out_specs=(whole, whole, whole),
        scratch_shapes=scratch,
        cost_estimate=pl.CostEstimate(
            flops=4 * rows * width * inner, bytes_accessed=4 * width * inner,
            transcendentals=rows * inner,
        ),
        compiler_params=pltpu.CompilerParams(
            collective_id=0, has_side_effects=True, vmem_limit_bytes=56 * 1024 * 1024
        ),
    )(
        caption_lengths, tokens, meta, image_embed, final_gain[None, :],
        up_weight[0], down_weight[0],
    )


def solution(mesh):
    split = P(("expert", "grid"), None)
    return jax.shard_map(
        on_device,
        mesh=mesh,
        in_specs=(split,) * 5 + (P(), P("expert", None, "grid"), P("expert", None, "grid")),
        out_specs=(split,) * 3,
        check_vma=False,
    )
```

```python
import functools
import math

import jax
import jax.numpy as jnp
from jax import lax
from jax.experimental import pallas as pl
from jax.experimental.pallas import tpu as pltpu
from jax.sharding import PartitionSpec as P

EPSILON = 1e-06
SIMILARITY_HEAT = 10.0
MESH = pl.DeviceIdType.MESH
BF16 = jnp.bfloat16
F32 = jnp.float32


def layer_norm(values):
    centred = values - jnp.mean(values, axis=-1, keepdims=True)
    return centred * lax.rsqrt(jnp.mean(centred * centred, axis=-1, keepdims=True) + EPSILON)


def root_norm(values):
    return values * lax.rsqrt(jnp.mean(values * values, axis=-1, keepdims=True) + EPSILON)


def flip(one, other, count):
    total, bit = 0, 1
    while bit < count:
        total = total + bit * (((one // bit) + (other // bit)) % 2)
        bit *= 2
    return total


def halves(values):
    high = values.astype(BF16)
    return high, (values - high.astype(F32)).astype(BF16)


def dot(left, right):
    return jnp.dot(left, right, preferred_element_type=F32)


def dot_nt(left, right):
    return lax.dot_general(left, right, (((1,), (1,)), ((), ())), preferred_element_type=F32)


def join(values, rows):
    width = values.shape[-1]
    if values.shape[-2] % 16 == 0:
        return values.reshape(rows, width)
    return values.astype(F32).reshape(rows, width).astype(values.dtype)


def part(values, lead):
    return values.reshape(lead + (values.shape[0] // math.prod(lead), values.shape[-1]))


def gelu(values):
    size = jnp.abs(values)
    t = 1.0 / (1.0 + (0.3275911 * math.sqrt(0.5)) * size)
    series = 0.5 * 1.061405429
    for term in (-1.453152027, 1.421413741, -0.284496736, 0.254829592):
        series = series * t + 0.5 * term
    tail = series * t * jnp.exp(values * values * -0.5)
    return jnp.maximum(values, 0.0) - size * tail


def slope(own, every, offset):
    logits = SIMILARITY_HEAT * dot_nt(own, every)
    row = lax.broadcasted_iota(jnp.int32, logits.shape, 0)
    column = lax.broadcasted_iota(jnp.int32, logits.shape, 1)
    signs = jnp.where(column == row + offset, 1.0, -1.0).astype(F32)
    coeff = -signs * jax.nn.sigmoid(-signs * logits)
    high, low = halves(coeff)
    return SIMILARITY_HEAT * (dot(high, every) + dot(low, every))


def kernel(
    experts, grids, slots, captions,
    lengths_ref, tokens_ref, routes_ref, gates_ref, image_ref, gain_ref, up_hbm, down_hbm,
    out_ref,
    up_ref, down_ref, send, gate_high, gate_low, rows, own, part_send, part_in, sum_send, sum_in,
    back_send, back_in, own_image, near_image, all_image, own_text, near_text, all_text,
    weight_sem, to_expert_s, to_expert_r, fx_s, fx_r, fc_s, fc_r, part_s, part_r, sum_s, sum_r,
    back_s, back_r, near_s, near_r, far_s, far_r,
):
    e = lax.axis_index("expert")
    g = lax.axis_index("grid")
    core = (e, g + 1 - 2 * (g % 2))
    cross = (e, (g + grids // 2) % grids)
    tokens, width = tokens_ref.shape
    group = grids * captions

    half = experts // 2

    def order(position):
        return position // 2 + (position % 2) * half

    def expert_peer(step):
        return (flip(e, order(step), experts), g)

    def push(source, target, send_sem, recv_sem, device):
        pltpu.make_async_remote_copy(
            src_ref=source, dst_ref=target, send_sem=send_sem, recv_sem=recv_sem,
            device_id=device, device_id_type=MESH,
        ).start()

    def await_bytes(ref, sem):
        pltpu.make_async_copy(ref, ref, sem).wait()

    barrier = pltpu.get_barrier_semaphore()

    def greet(step, carry):
        pl.semaphore_signal(barrier, inc=1, device_id=expert_peer(step), device_id_type=MESH)
        return carry

    lax.fori_loop(1, experts, greet, 0)
    for hop in range(1, grids):
        pl.semaphore_signal(barrier, inc=1, device_id=(e, (g + hop) % grids), device_id_type=MESH)
    load_up = pltpu.make_async_copy(up_hbm, up_ref, weight_sem.at[0])
    load_up.start()
    load_down = pltpu.make_async_copy(down_hbm, down_ref, weight_sem.at[1])
    load_down.start()

    normed = layer_norm(tokens_ref[...].astype(F32)).astype(BF16)
    routes = routes_ref[...]
    first, second = routes[0:1, :], routes[1:2, :]
    ids = lax.broadcasted_iota(jnp.int32, (max(experts, 8), tokens), 0)
    named = ((ids == first) | (ids == second)).astype(F32).astype(BF16)
    before = lax.broadcasted_iota(jnp.int32, (tokens, tokens), 0)
    after = lax.broadcasted_iota(jnp.int32, (tokens, tokens), 1)
    ranks = dot(named, (before < after).astype(F32).astype(BF16))
    spots = lax.broadcasted_iota(jnp.int32, (experts * slots, tokens), 0)
    taken = None
    weights = None
    for choice, chosen in enumerate((first, second)):
        rank = jnp.sum(jnp.where(ids == chosen, ranks, 0.0), axis=0, keepdims=True)
        far = flip(chosen, e, experts)
        place = (2 * (far % half) + far // half) * slots + rank.astype(jnp.int32)
        hit = spots == place
        weight = jnp.where(hit, gates_ref[choice:choice + 1, :], 0.0)
        taken = hit if taken is None else taken | hit
        weights = weight if weights is None else weights + weight
    blocks = part(dot(taken.astype(F32).astype(BF16), normed), (experts,)).astype(BF16)
    send[...] = blocks
    rows[0, 0] = blocks[0]
    high, low = halves(weights.T)
    gate_high[...] = high
    gate_low[...] = low

    line = lax.broadcasted_iota(jnp.int32, (2 * group, 1), 0)
    caption = jnp.where(line < group, line - g * captions, line - group)
    images = root_norm(image_ref[...].astype(F32)) / math.sqrt(width)
    spread = jnp.zeros((2 * group, width), F32)
    for index in range(captions):
        spread = jnp.where(caption == index, images[index:index + 1, :], spread)
    near_image[0] = spread[:group].astype(BF16)
    own_image[...] = spread[group:].astype(BF16)

    pl.semaphore_wait(barrier, experts + grids - 2)

    def dispatch(step, carry):
        push(send.at[step], rows.at[step, 0], to_expert_s, to_expert_r.at[step], expert_peer(step))
        return carry

    lax.fori_loop(1, experts, dispatch, 0)

    def share_near(near, index):
        for hop in range(1, grids):
            push(near.at[0], near.at[hop], near_s.at[index], near_r.at[index], (e, (g + hop) % grids))

    def share_far(near, every, index):
        await_bytes(near.at[pl.ds(1, grids - 1)], near_r.at[index])
        total = near[0].astype(F32)
        for hop in range(1, grids):
            total = total + near[hop].astype(F32)
        every[0] = total.astype(BF16)

        def each(step, carry):
            push(every.at[0], every.at[step], far_s.at[index], far_r.at[index], expert_peer(step))
            return carry

        lax.fori_loop(1, experts, each, 0)

    share_near(near_image, 0)

    def turn(index, carry):
        @pl.when(index < experts)
        def _():
            at = index

            @pl.when(at > 0)
            def _():
                await_bytes(rows.at[at, 0], to_expert_r.at[at])

            push(rows.at[at, 0], rows.at[at, 1], fx_s, fx_r.at[at], cross)
            push(rows.at[at, 0], rows.at[at, 2], fc_s, fc_r.at[at], core)

        @pl.when((index >= 1) & (index < experts + 1))
        def _():
            at = index - 1
            await_bytes(rows.at[at, 1], fx_r.at[at])
            push(rows.at[at, 1], rows.at[at, 3], fc_s, fc_r.at[at], core)

        @pl.when(index == 1)
        def _():
            share_far(near_image, all_image, 0)
            load_up.wait()
            load_down.wait()

        @pl.when((index >= 2) & (index < experts + 2))
        def _():
            at = index - 2
            await_bytes(rows.at[at, pl.ds(2, 2)], fc_r.at[at])
            block = join(rows[at], grids * slots)
            tile = up_ref.shape[1] // 4
            parts = [
                gelu(dot(block, up_ref[:, low:low + tile])).astype(BF16)
                for low in range(0, 4 * tile, tile)
            ]
            term = part(dot_nt(jnp.concatenate(parts, axis=1), down_ref[...]), (grids,))
            own[at] = term[:2]
            part_send[at] = term[2:].astype(BF16)
            push(part_send.at[at], part_in.at[at], part_s, part_r.at[at], core)

        @pl.when((index >= 3) & (index < experts + 3))
        def _():
            at = index - 3
            await_bytes(part_in.at[at], part_r.at[at])
            sum_send[at] = (own[at, 1] + part_in[at, 1].astype(F32)).astype(BF16)
            push(sum_send.at[at], sum_in.at[at], sum_s, sum_r.at[at], cross)

        @pl.when(index >= 4)
        def _():
            at = index - 4
            await_bytes(sum_in.at[at], sum_r.at[at])
            result = own[at, 0] + part_in[at, 0].astype(F32) + sum_in[at].astype(F32)

            @pl.when(at == 0)
            def _():
                back_in[0] = result.astype(BF16)

            @pl.when(at > 0)
            def _():
                back_send[at] = result.astype(BF16)
                push(back_send.at[at], back_in.at[at], back_s, back_r, expert_peer(at))

        return carry

    lax.fori_loop(0, experts + 4, turn, 0)

    await_bytes(back_in.at[pl.ds(1, experts - 1)], back_r)
    returned = join(back_in[...], experts * slots)
    picked = dot(gate_high[...], returned) + dot(gate_low[...], returned)
    final = layer_norm(tokens_ref[...].astype(F32) + picked) * gain_ref[...]
    starts = jnp.zeros((2 * group, 1), jnp.int32)
    ends = jnp.zeros((2 * group, 1), jnp.int32)
    reached = 0
    for index in range(captions):
        starts = jnp.where(caption == index, reached, starts)
        reached = reached + lengths_ref[0, index]
        ends = jnp.where(caption == index, reached, ends)
    spot = lax.broadcasted_iota(jnp.int32, (2 * group, tokens), 1)
    members = ((spot >= starts) & (spot < ends)).astype(F32).astype(BF16)
    high, low = halves(final)
    pooled = (dot(members, high) + dot(members, low)) / jnp.maximum(ends - starts, 1).astype(F32)
    embed = root_norm(pooled)
    out_ref[0] = embed[group:group + captions]
    direction = embed / math.sqrt(width)
    near_text[0] = direction[:group].astype(BF16)
    own_text[...] = direction[group:].astype(BF16)
    share_near(near_text, 1)
    share_far(near_text, all_text, 1)

    others = pl.ds(1, experts - 1)
    await_bytes(all_image.at[others], far_r.at[0])
    images_all = all_image[...].reshape(experts * group, width)
    offset = g * captions
    out_ref[1] = slope(own_text[...], images_all, offset)[:captions]
    await_bytes(all_text.at[others], far_r.at[1])
    texts_all = all_text[...].reshape(experts * group, width)
    out_ref[2] = slope(own_image[...], texts_all, offset)[:captions]

    await_bytes(send.at[others], to_expert_s)
    await_bytes(send, fx_s)
    await_bytes(part_send, fc_s)
    await_bytes(part_send, part_s)
    await_bytes(sum_send, sum_s)
    await_bytes(back_send.at[others], back_s)
    for index, (near, every) in enumerate(((near_image, all_image), (near_text, all_text))):
        await_bytes(near.at[pl.ds(1, grids - 1)], near_s.at[index])
        await_bytes(every.at[others], far_s.at[index])


def on_device(
    tokens, routes, route_gates, caption_lengths, image_embed, final_gain, up_weight, down_weight
):
    count, width = tokens.shape
    experts, grids = lax.axis_size("expert"), lax.axis_size("grid")
    slots = 4 * count // experts
    captions = caption_lengths.shape[1]
    group = grids * captions
    inner = up_weight.shape[2]
    dma = pltpu.SemaphoreType.DMA
    whole = pl.BlockSpec(memory_space=pltpu.VMEM)
    far = pl.BlockSpec(memory_space=pl.ANY)
    out = jax.ShapeDtypeStruct((3, captions, width), F32)
    scratch = [
        pltpu.VMEM((width, inner), BF16),
        pltpu.VMEM((width, inner), BF16),
        pltpu.VMEM((experts, slots, width), BF16),
        pltpu.VMEM((count, experts * slots), BF16),
        pltpu.VMEM((count, experts * slots), BF16),
        pltpu.VMEM((experts, grids, slots, width), BF16),
        pltpu.VMEM((experts, 2, slots, width), F32),
        pltpu.VMEM((experts, 2, slots, width), BF16),
        pltpu.VMEM((experts, 2, slots, width), BF16),
    ] + [pltpu.VMEM((experts, slots, width), BF16)] * 4 + [
        pltpu.VMEM((group, width), BF16),
        pltpu.VMEM((grids, group, width), BF16),
        pltpu.VMEM((experts, group, width), BF16),
    ] * 2 + [
        dma((2,)),
        dma, dma((experts,)),
        dma, dma((experts,)),
        dma, dma((experts,)),
        dma, dma((experts,)),
        dma, dma((experts,)),
        dma, dma,
        dma((2,)), dma((2,)), dma((2,)), dma((2,)),
    ]
    rows = experts * slots * grids
    result = pl.pallas_call(
        functools.partial(kernel, experts, grids, slots, captions),
        out_shape=out,
        in_specs=[pl.BlockSpec(memory_space=pltpu.SMEM)] + [whole] * 5 + [far] * 2,
        out_specs=whole,
        scratch_shapes=scratch,
        cost_estimate=pl.CostEstimate(
            flops=4 * rows * width * inner, bytes_accessed=4 * width * inner,
            transcendentals=rows * inner,
        ),
        compiler_params=pltpu.CompilerParams(
            collective_id=0, has_side_effects=True, vmem_limit_bytes=56 * 1024 * 1024
        ),
    )(
        caption_lengths, tokens, routes.T, route_gates.T, image_embed, final_gain[None, :],
        up_weight[0], down_weight[0],
    )
    return result[0], result[1], result[2]


def solution(mesh):
    split = P(("expert", "grid"), None)
    return jax.shard_map(
        on_device,
        mesh=mesh,
        in_specs=(split,) * 5 + (P(), P("expert", None, "grid"), P("expert", None, "grid")),
        out_specs=(split,) * 3,
        check_vma=False,
    )
```

```python
import functools
import math

import jax
import jax.numpy as jnp
from jax import lax
from jax.experimental import pallas as pl
from jax.experimental.pallas import tpu as pltpu
from jax.sharding import PartitionSpec as P

EPSILON = 1e-06
SIMILARITY_HEAT = 10.0
MESH = pl.DeviceIdType.MESH
BF16 = jnp.bfloat16
F32 = jnp.float32


def layer_norm(values):
    centred = values - jnp.mean(values, axis=-1, keepdims=True)
    return centred * lax.rsqrt(jnp.mean(centred * centred, axis=-1, keepdims=True) + EPSILON)


def root_norm(values):
    return values * lax.rsqrt(jnp.mean(values * values, axis=-1, keepdims=True) + EPSILON)


def flip(one, other, count):
    total, bit = 0, 1
    while bit < count:
        total = total + bit * (((one // bit) + (other // bit)) % 2)
        bit *= 2
    return total


def halves(values):
    high = values.astype(BF16)
    return high, (values - high.astype(F32)).astype(BF16)


def dot(left, right):
    return jnp.dot(left, right, preferred_element_type=F32)


def dot_nt(left, right):
    return lax.dot_general(left, right, (((1,), (1,)), ((), ())), preferred_element_type=F32)


def join(values, rows):
    width = values.shape[-1]
    if values.shape[-2] % 16 == 0:
        return values.reshape(rows, width)
    return values.astype(F32).reshape(rows, width).astype(values.dtype)


def part(values, lead):
    return values.reshape(lead + (values.shape[0] // math.prod(lead), values.shape[-1]))


def gelu(values):
    size = jnp.abs(values)
    t = 1.0 / (1.0 + (0.3275911 * math.sqrt(0.5)) * size)
    series = 0.5 * 1.061405429
    for term in (-1.453152027, 1.421413741, -0.284496736, 0.254829592):
        series = series * t + 0.5 * term
    tail = series * t * jnp.exp(values * values * -0.5)
    return jnp.maximum(values, 0.0) - size * tail


def slope(own, every, offset):
    logits = SIMILARITY_HEAT * dot_nt(own, every)
    row = lax.broadcasted_iota(jnp.int32, logits.shape, 0)
    column = lax.broadcasted_iota(jnp.int32, logits.shape, 1)
    signs = jnp.where(column == row + offset, 1.0, -1.0).astype(F32)
    coeff = -signs * jax.nn.sigmoid(-signs * logits)
    high, low = halves(coeff)
    return SIMILARITY_HEAT * (dot(high, every) + dot(low, every))


def kernel(
    experts, grids, slots, captions,
    lengths_ref, tokens_ref, routes_ref, gates_ref, image_ref, gain_ref, up_hbm, down_hbm,
    out_ref,
    up_ref, down_ref, send, gate_high, gate_low, rows, own, part_send, part_in, sum_send, sum_in,
    back_send, back_in, own_image, near_image, all_image, own_text, near_text, all_text,
    weight_sem, to_expert_s, to_expert_r, fx_s, fx_r, fc_s, fc_r, part_s, part_r, sum_s, sum_r,
    back_s, back_r, near_s, near_r, far_s, far_r,
):
    e = lax.axis_index("expert")
    g = lax.axis_index("grid")
    core = (e, g + 1 - 2 * (g % 2))
    cross = (e, (g + grids // 2) % grids)
    tokens, width = tokens_ref.shape
    group = grids * captions

    half = experts // 2

    def order(position):
        turned = position + experts - 1
        turn_of = turned % experts
        pair, odd = turn_of // 2 + 1, turn_of % 2
        return (turned // experts) * ((1 - odd) * pair + odd * (half + pair % half))

    def expert_peer(step):
        return (flip(e, order(step), experts), g)

    def push(source, target, send_sem, recv_sem, device):
        pltpu.make_async_remote_copy(
            src_ref=source, dst_ref=target, send_sem=send_sem, recv_sem=recv_sem,
            device_id=device, device_id_type=MESH,
        ).start()

    def await_bytes(ref, sem):
        pltpu.make_async_copy(ref, ref, sem).wait()

    barrier = pltpu.get_barrier_semaphore()

    def greet(step, carry):
        pl.semaphore_signal(barrier, inc=1, device_id=expert_peer(step), device_id_type=MESH)
        return carry

    lax.fori_loop(1, experts, greet, 0)
    for hop in range(1, grids):
        pl.semaphore_signal(barrier, inc=1, device_id=(e, (g + hop) % grids), device_id_type=MESH)
    load_up = pltpu.make_async_copy(up_hbm, up_ref, weight_sem.at[0])
    load_up.start()
    load_down = pltpu.make_async_copy(down_hbm, down_ref, weight_sem.at[1])
    load_down.start()

    normed = layer_norm(tokens_ref[...].astype(F32)).astype(BF16)
    routes = routes_ref[...]
    first, second = routes[0:1, :], routes[1:2, :]
    ids = lax.broadcasted_iota(jnp.int32, (max(experts, 8), tokens), 0)
    named = ((ids == first) | (ids == second)).astype(F32).astype(BF16)
    before = lax.broadcasted_iota(jnp.int32, (tokens, tokens), 0)
    after = lax.broadcasted_iota(jnp.int32, (tokens, tokens), 1)
    ranks = dot(named, (before < after).astype(F32).astype(BF16))
    spots = lax.broadcasted_iota(jnp.int32, (experts * slots, tokens), 0)
    hits = []
    for chosen in (first, second):
        rank = jnp.sum(jnp.where(ids == chosen, ranks, 0.0), axis=0, keepdims=True)
        far = flip(chosen, e, experts)
        spot_of = jnp.where(far > half, 2 * (far - half), jnp.maximum(2 * far - 1, 0))
        hits.append(spots == spot_of * slots + rank.astype(jnp.int32))
    taken = (hits[0] | hits[1]).astype(F32).astype(BF16)
    blocks = part(dot(taken, normed), (experts,)).astype(BF16)
    send[...] = blocks
    rows[0, 0] = blocks[0]
    pl.semaphore_wait(barrier, experts + grids - 2)

    def dispatch(step, carry):
        push(send.at[step], rows.at[step, 0], to_expert_s, to_expert_r.at[step], expert_peer(step))
        return carry

    ahead = min(3, experts)
    lax.fori_loop(1, ahead, dispatch, 0)
    push(rows.at[0, 0], rows.at[0, 1], fx_s, fx_r.at[0], cross)
    push(rows.at[0, 0], rows.at[0, 2], fc_s, fc_r.at[0], core)
    weights = jnp.where(hits[0], gates_ref[0:1, :], 0.0) + jnp.where(hits[1], gates_ref[1:2, :], 0.0)
    high, low = halves(weights.T)
    gate_high[...] = high
    gate_low[...] = low

    line = lax.broadcasted_iota(jnp.int32, (2 * group, 1), 0)
    caption = jnp.where(line < group, line - g * captions, line - group)
    images = root_norm(image_ref[...].astype(F32)) / math.sqrt(width)
    spread = jnp.zeros((2 * group, width), F32)
    for index in range(captions):
        spread = jnp.where(caption == index, images[index:index + 1, :], spread)
    near_image[0] = spread[:group].astype(BF16)
    own_image[...] = spread[group:].astype(BF16)

    def share_near(near, index):
        for hop in range(1, grids):
            push(near.at[0], near.at[hop], near_s.at[index], near_r.at[index], (e, (g + hop) % grids))

    def share_far(near, every, index):
        await_bytes(near.at[pl.ds(1, grids - 1)], near_r.at[index])
        total = near[0].astype(F32)
        for hop in range(1, grids):
            total = total + near[hop].astype(F32)
        every[0] = total.astype(BF16)

        def each(step, carry):
            push(every.at[0], every.at[step], far_s.at[index], far_r.at[index], expert_peer(step))
            return carry

        lax.fori_loop(1, experts, each, 0)

    share_near(near_image, 0)

    def turn(index, carry):
        @pl.when(index + ahead < experts)
        def _():
            dispatch(index + ahead, 0)

        @pl.when((index > 0) & (index < experts))
        def _():
            at = index
            await_bytes(rows.at[at, 0], to_expert_r.at[at])
            push(rows.at[at, 0], rows.at[at, 1], fx_s, fx_r.at[at], cross)
            push(rows.at[at, 0], rows.at[at, 2], fc_s, fc_r.at[at], core)

        @pl.when((index >= 1) & (index < experts + 1))
        def _():
            at = index - 1
            await_bytes(rows.at[at, 1], fx_r.at[at])
            push(rows.at[at, 1], rows.at[at, 3], fc_s, fc_r.at[at], core)

        @pl.when(index == 1)
        def _():
            share_far(near_image, all_image, 0)
            load_up.wait()
            load_down.wait()

        @pl.when((index >= 2) & (index < experts + 2))
        def _():
            at = index - 2
            await_bytes(rows.at[at, pl.ds(2, 2)], fc_r.at[at])
            block = join(rows[at], grids * slots)
            tile = up_ref.shape[1] // 4
            parts = [
                gelu(dot(block, up_ref[:, low:low + tile])).astype(BF16)
                for low in range(0, 4 * tile, tile)
            ]
            term = part(dot_nt(jnp.concatenate(parts, axis=1), down_ref[...]), (grids,))
            own[at] = term[:2]
            part_send[at] = term[2:].astype(BF16)
            push(part_send.at[at], part_in.at[at], part_s, part_r.at[at], core)

        @pl.when((index >= 3) & (index < experts + 3))
        def _():
            at = index - 3
            await_bytes(part_in.at[at], part_r.at[at])
            sum_send[at] = (own[at, 1] + part_in[at, 1].astype(F32)).astype(BF16)
            push(sum_send.at[at], sum_in.at[at], sum_s, sum_r.at[at], cross)

        @pl.when(index >= 4)
        def _():
            at = index - 4
            await_bytes(sum_in.at[at], sum_r.at[at])
            result = own[at, 0] + part_in[at, 0].astype(F32) + sum_in[at].astype(F32)

            @pl.when(at == 0)
            def _():
                back_in[0] = result.astype(BF16)

            @pl.when(at > 0)
            def _():
                back_send[at] = result.astype(BF16)
                push(back_send.at[at], back_in.at[at], back_s, back_r, expert_peer(at))

        return carry

    lax.fori_loop(0, experts + 4, turn, 0)

    await_bytes(back_in.at[pl.ds(1, experts - 1)], back_r)
    returned = join(back_in[...], experts * slots)
    picked = dot(gate_high[...], returned) + dot(gate_low[...], returned)
    final = layer_norm(tokens_ref[...].astype(F32) + picked) * gain_ref[...]
    starts = jnp.zeros((2 * group, 1), jnp.int32)
    ends = jnp.zeros((2 * group, 1), jnp.int32)
    reached = 0
    for index in range(captions):
        starts = jnp.where(caption == index, reached, starts)
        reached = reached + lengths_ref[0, index]
        ends = jnp.where(caption == index, reached, ends)
    spot = lax.broadcasted_iota(jnp.int32, (2 * group, tokens), 1)
    members = ((spot >= starts) & (spot < ends)).astype(F32).astype(BF16)
    high, low = halves(final)
    pooled = (dot(members, high) + dot(members, low)) / jnp.maximum(ends - starts, 1).astype(F32)
    embed = root_norm(pooled)
    out_ref[0] = embed[group:group + captions]
    direction = embed / math.sqrt(width)
    near_text[0] = direction[:group].astype(BF16)
    own_text[...] = direction[group:].astype(BF16)
    share_near(near_text, 1)
    share_far(near_text, all_text, 1)

    others = pl.ds(1, experts - 1)
    await_bytes(all_image.at[others], far_r.at[0])
    images_all = all_image[...].reshape(experts * group, width)
    offset = g * captions
    out_ref[1] = slope(own_text[...], images_all, offset)[:captions]
    await_bytes(all_text.at[others], far_r.at[1])
    texts_all = all_text[...].reshape(experts * group, width)
    out_ref[2] = slope(own_image[...], texts_all, offset)[:captions]

    await_bytes(send.at[others], to_expert_s)
    await_bytes(send, fx_s)
    await_bytes(part_send, fc_s)
    await_bytes(part_send, part_s)
    await_bytes(sum_send, sum_s)
    await_bytes(back_send.at[others], back_s)
    for index, (near, every) in enumerate(((near_image, all_image), (near_text, all_text))):
        await_bytes(near.at[pl.ds(1, grids - 1)], near_s.at[index])
        await_bytes(every.at[others], far_s.at[index])


def on_device(
    tokens, routes, route_gates, caption_lengths, image_embed, final_gain, up_weight, down_weight
):
    count, width = tokens.shape
    experts, grids = lax.axis_size("expert"), lax.axis_size("grid")
    slots = 4 * count // experts
    captions = caption_lengths.shape[1]
    group = grids * captions
    inner = up_weight.shape[2]
    dma = pltpu.SemaphoreType.DMA
    whole = pl.BlockSpec(memory_space=pltpu.VMEM)
    far = pl.BlockSpec(memory_space=pl.ANY)
    out = jax.ShapeDtypeStruct((3, captions, width), F32)
    scratch = [
        pltpu.VMEM((width, inner), BF16),
        pltpu.VMEM((width, inner), BF16),
        pltpu.VMEM((experts, slots, width), BF16),
        pltpu.VMEM((count, experts * slots), BF16),
        pltpu.VMEM((count, experts * slots), BF16),
        pltpu.VMEM((experts, grids, slots, width), BF16),
        pltpu.VMEM((experts, 2, slots, width), F32),
        pltpu.VMEM((experts, 2, slots, width), BF16),
        pltpu.VMEM((experts, 2, slots, width), BF16),
    ] + [pltpu.VMEM((experts, slots, width), BF16)] * 4 + [
        pltpu.VMEM((group, width), BF16),
        pltpu.VMEM((grids, group, width), BF16),
        pltpu.VMEM((experts, group, width), BF16),
    ] * 2 + [
        dma((2,)),
        dma, dma((experts,)),
        dma, dma((experts,)),
        dma, dma((experts,)),
        dma, dma((experts,)),
        dma, dma((experts,)),
        dma, dma,
        dma((2,)), dma((2,)), dma((2,)), dma((2,)),
    ]
    rows = experts * slots * grids
    result = pl.pallas_call(
        functools.partial(kernel, experts, grids, slots, captions),
        out_shape=out,
        in_specs=[pl.BlockSpec(memory_space=pltpu.SMEM)] + [whole] * 5 + [far] * 2,
        out_specs=whole,
        scratch_shapes=scratch,
        cost_estimate=pl.CostEstimate(
            flops=4 * rows * width * inner, bytes_accessed=4 * width * inner,
            transcendentals=rows * inner,
        ),
        compiler_params=pltpu.CompilerParams(
            collective_id=0, has_side_effects=True, vmem_limit_bytes=56 * 1024 * 1024
        ),
    )(
        caption_lengths, tokens, routes.T, route_gates.T, image_embed, final_gain[None, :],
        up_weight[0], down_weight[0],
    )
    return result[0], result[1], result[2]


def solution(mesh):
    split = P(("expert", "grid"), None)
    return jax.shard_map(
        on_device,
        mesh=mesh,
        in_specs=(split,) * 5 + (P(), P("expert", None, "grid"), P("expert", None, "grid")),
        out_specs=(split,) * 3,
        check_vma=False,
    )
```

```python
import functools
import math

import jax
import jax.numpy as jnp
from jax import lax
from jax.experimental import pallas as pl
from jax.experimental.pallas import tpu as pltpu
from jax.sharding import PartitionSpec as P

EPSILON = 1e-06
SIMILARITY_HEAT = 10.0
MESH = pl.DeviceIdType.MESH
BF16 = jnp.bfloat16
F32 = jnp.float32


def layer_norm(values):
    centred = values - jnp.mean(values, axis=-1, keepdims=True)
    return centred * lax.rsqrt(jnp.mean(centred * centred, axis=-1, keepdims=True) + EPSILON)


def root_norm(values):
    return values * lax.rsqrt(jnp.mean(values * values, axis=-1, keepdims=True) + EPSILON)


def flip(one, other, count):
    total, bit = 0, 1
    while bit < count:
        total = total + bit * (((one // bit) + (other // bit)) % 2)
        bit *= 2
    return total


def halves(values):
    high = values.astype(BF16)
    return high, (values - high.astype(F32)).astype(BF16)


def dot(left, right):
    return jnp.dot(left, right, preferred_element_type=F32)


def dot_nt(left, right):
    return lax.dot_general(left, right, (((1,), (1,)), ((), ())), preferred_element_type=F32)


def join(values, rows):
    width = values.shape[-1]
    if values.shape[-2] % 16 == 0:
        return values.reshape(rows, width)
    return values.astype(F32).reshape(rows, width).astype(values.dtype)


def part(values, lead):
    return values.reshape(lead + (values.shape[0] // math.prod(lead), values.shape[-1]))


def gelu(values):
    size = jnp.abs(values)
    t = 1.0 / (1.0 + (0.3275911 * math.sqrt(0.5)) * size)
    series = 0.5 * 1.061405429
    for term in (-1.453152027, 1.421413741, -0.284496736, 0.254829592):
        series = series * t + 0.5 * term
    tail = series * t * jnp.exp(values * values * -0.5)
    return jnp.maximum(values, 0.0) - size * tail


def slope(own, every, offset):
    logits = SIMILARITY_HEAT * dot_nt(own, every)
    row = lax.broadcasted_iota(jnp.int32, logits.shape, 0)
    column = lax.broadcasted_iota(jnp.int32, logits.shape, 1)
    signs = jnp.where(column == row + offset, 1.0, -1.0).astype(F32)
    coeff = -signs * jax.nn.sigmoid(-signs * logits)
    high, low = halves(coeff)
    return SIMILARITY_HEAT * (dot(high, every) + dot(low, every))


def kernel(
    experts, grids, slots, captions,
    lengths_ref, tokens_ref, routes_ref, gates_ref, image_ref, gain_ref, up_hbm, down_hbm,
    out_ref,
    up_ref, down_ref, down_turned, send, gate_high, gate_low, rows, own, part_send, part_in, sum_send, sum_in,
    back_send, back_in, own_image, near_image, all_image, own_text, near_text, all_text,
    weight_sem, to_expert_s, to_expert_r, fx_s, fx_r, fc_s, fc_r, part_s, part_r, sum_s, sum_r,
    back_s, back_r, near_s, near_r, far_s, far_r, across_r, spread_r,
):
    e = lax.axis_index("expert")
    g = lax.axis_index("grid")
    core = (e, g + 1 - 2 * (g % 2))
    cross = (e, (g + grids // 2) % grids)
    tokens, width = tokens_ref.shape
    group = grids * captions

    half = experts // 2

    def order(position):
        turned = position + experts - 1
        turn_of = turned % experts
        pair, odd = turn_of // 2 + 1, turn_of % 2
        return (turned // experts) * ((1 - odd) * pair + odd * (half + pair % half))

    opposite = ((e + half) % experts, g)

    def near_peer(step):
        return (flip(e, step, experts), g)

    def expert_peer(step):
        return (flip(e, order(step), experts), g)

    def push(source, target, send_sem, recv_sem, device):
        pltpu.make_async_remote_copy(
            src_ref=source, dst_ref=target, send_sem=send_sem, recv_sem=recv_sem,
            device_id=device, device_id_type=MESH,
        ).start()

    def await_bytes(ref, sem):
        pltpu.make_async_copy(ref, ref, sem).wait()

    barrier = pltpu.get_barrier_semaphore()

    def greet(step, carry):
        pl.semaphore_signal(barrier, inc=1, device_id=expert_peer(step), device_id_type=MESH)
        return carry

    lax.fori_loop(1, experts, greet, 0)
    for hop in range(1, grids):
        pl.semaphore_signal(barrier, inc=1, device_id=(e, (g + hop) % grids), device_id_type=MESH)
    load_up = pltpu.make_async_copy(up_hbm, up_ref, weight_sem.at[0])
    load_up.start()
    load_down = pltpu.make_async_copy(down_hbm, down_ref, weight_sem.at[1])
    load_down.start()

    normed = layer_norm(tokens_ref[...].astype(F32)).astype(BF16)
    routes = routes_ref[...]
    first, second = routes[0:1, :], routes[1:2, :]
    ids = lax.broadcasted_iota(jnp.int32, (max(experts, 8), tokens), 0)
    named = ((ids == first) | (ids == second)).astype(F32).astype(BF16)
    before = lax.broadcasted_iota(jnp.int32, (tokens, tokens), 0)
    after = lax.broadcasted_iota(jnp.int32, (tokens, tokens), 1)
    ranks = dot(named, (before < after).astype(F32).astype(BF16))
    spots = lax.broadcasted_iota(jnp.int32, (experts * slots, tokens), 0)
    hits = []
    for chosen in (first, second):
        rank = jnp.sum(jnp.where(ids == chosen, ranks, 0.0), axis=0, keepdims=True)
        far = flip(chosen, e, experts)
        spot_of = jnp.where(far > half, 2 * (far - half), jnp.maximum(2 * far - 1, 0))
        hits.append(spots == spot_of * slots + rank.astype(jnp.int32))
    taken = (hits[0] | hits[1]).astype(F32).astype(BF16)
    blocks = part(dot(taken, normed), (experts,)).astype(BF16)
    send[...] = blocks
    rows[0, 0] = blocks[0]
    pl.semaphore_wait(barrier, experts + grids - 2)

    def dispatch(step, carry):
        push(send.at[step], rows.at[step, 0], to_expert_s, to_expert_r.at[step], expert_peer(step))
        return carry

    ahead = min(3, experts)
    lax.fori_loop(1, ahead, dispatch, 0)
    push(rows.at[0, 0], rows.at[0, 1], fx_s, fx_r.at[0], cross)
    push(rows.at[0, 0], rows.at[0, 2], fc_s, fc_r.at[0], core)
    weights = jnp.where(hits[0], gates_ref[0:1, :], 0.0) + jnp.where(hits[1], gates_ref[1:2, :], 0.0)
    high, low = halves(weights.T)
    gate_high[...] = high
    gate_low[...] = low

    line = lax.broadcasted_iota(jnp.int32, (2 * group, 1), 0)
    caption = jnp.where(line < group, line - g * captions, line - group)
    images = root_norm(image_ref[...].astype(F32)) / math.sqrt(width)
    spread = jnp.zeros((2 * group, width), F32)
    for index in range(captions):
        spread = jnp.where(caption == index, images[index:index + 1, :], spread)
    near_image[0] = spread[:group].astype(BF16)
    own_image[...] = spread[group:].astype(BF16)

    def share_near(near, index):
        for hop in range(1, grids):
            push(near.at[0], near.at[hop], near_s.at[index], near_r.at[index], (e, (g + hop) % grids))

    def share_far(near, every, index):
        await_bytes(near.at[pl.ds(1, grids - 1)], near_r.at[index])
        total = near[0].astype(F32)
        for hop in range(1, grids):
            total = total + near[hop].astype(F32)
        every[0] = total.astype(BF16)

        push(every.at[0], every.at[half], far_s.at[index], across_r.at[index], opposite)

        def each(step, carry):
            push(every.at[0], every.at[step], far_s.at[index], far_r.at[index], near_peer(step))
            return carry

        lax.fori_loop(1, half, each, 0)

    def spread_far(every, index):
        await_bytes(every.at[half], across_r.at[index])

        def each(step, carry):
            push(
                every.at[half], every.at[half + step], far_s.at[index], spread_r.at[index],
                near_peer(step),
            )
            return carry

        lax.fori_loop(1, half, each, 0)

    def await_far(every, index):
        await_bytes(every.at[pl.ds(1, half - 1)], far_r.at[index])
        await_bytes(every.at[pl.ds(half + 1, half - 1)], spread_r.at[index])

    share_near(near_image, 0)

    tile = up_ref.shape[1] // 4

    def turn(index, carry):
        @pl.when(index + ahead < experts)
        def _():
            dispatch(index + ahead, 0)

        @pl.when((index > 0) & (index < experts))
        def _():
            at = index
            await_bytes(rows.at[at, 0], to_expert_r.at[at])
            push(rows.at[at, 0], rows.at[at, 1], fx_s, fx_r.at[at], cross)
            push(rows.at[at, 0], rows.at[at, 2], fc_s, fc_r.at[at], core)

        @pl.when((index >= 1) & (index < experts + 1))
        def _():
            at = index - 1
            await_bytes(rows.at[at, 1], fx_r.at[at])
            push(rows.at[at, 1], rows.at[at, 3], fc_s, fc_r.at[at], core)

        @pl.when(index == 1)
        def _():
            share_far(near_image, all_image, 0)
            load_up.wait()
            load_down.wait()
            for low in range(0, 4 * tile, tile):
                down_turned[low:low + tile] = down_ref[:, low:low + tile].T

        @pl.when((index >= 2) & (index < experts + 2))
        def _():
            at = index - 2
            await_bytes(rows.at[at, pl.ds(2, 2)], fc_r.at[at])
            block = join(rows[at], grids * slots)
            parts = [
                gelu(dot(block, up_ref[:, low:low + tile])).astype(BF16)
                for low in range(0, 4 * tile, tile)
            ]
            term = part(dot(jnp.concatenate(parts, axis=1), down_turned[...]), (grids,))
            own[at] = term[:2]
            part_send[at] = term[2:].astype(BF16)
            push(part_send.at[at], part_in.at[at], part_s, part_r.at[at], core)

        @pl.when(index == 3)
        def _():
            spread_far(all_image, 0)

        @pl.when((index >= 3) & (index < experts + 3))
        def _():
            at = index - 3
            await_bytes(part_in.at[at], part_r.at[at])
            sum_send[at] = (own[at, 1] + part_in[at, 1].astype(F32)).astype(BF16)
            push(sum_send.at[at], sum_in.at[at], sum_s, sum_r.at[at], cross)

        @pl.when(index >= 4)
        def _():
            at = index - 4
            await_bytes(sum_in.at[at], sum_r.at[at])
            result = own[at, 0] + part_in[at, 0].astype(F32) + sum_in[at].astype(F32)

            @pl.when(at == 0)
            def _():
                back_in[0] = result.astype(BF16)

            @pl.when(at > 0)
            def _():
                back_send[at] = result.astype(BF16)
                push(back_send.at[at], back_in.at[at], back_s, back_r, expert_peer(at))

        return carry

    lax.fori_loop(0, experts + 4, turn, 0)

    await_bytes(back_in.at[pl.ds(1, experts - 1)], back_r)
    returned = join(back_in[...], experts * slots)
    picked = dot(gate_high[...], returned) + dot(gate_low[...], returned)
    final = layer_norm(tokens_ref[...].astype(F32) + picked) * gain_ref[...]
    starts = jnp.zeros((2 * group, 1), jnp.int32)
    ends = jnp.zeros((2 * group, 1), jnp.int32)
    reached = 0
    for index in range(captions):
        starts = jnp.where(caption == index, reached, starts)
        reached = reached + lengths_ref[0, index]
        ends = jnp.where(caption == index, reached, ends)
    spot = lax.broadcasted_iota(jnp.int32, (2 * group, tokens), 1)
    members = ((spot >= starts) & (spot < ends)).astype(F32).astype(BF16)
    high, low = halves(final)
    pooled = (dot(members, high) + dot(members, low)) / jnp.maximum(ends - starts, 1).astype(F32)
    embed = root_norm(pooled)
    out_ref[0] = embed[group:group + captions]
    direction = embed / math.sqrt(width)
    near_text[0] = direction[:group].astype(BF16)
    own_text[...] = direction[group:].astype(BF16)
    share_near(near_text, 1)
    share_far(near_text, all_text, 1)

    others = pl.ds(1, experts - 1)
    spread_far(all_text, 1)
    await_far(all_image, 0)
    images_all = all_image[...].reshape(experts * group, width)
    offset = g * captions
    out_ref[1] = slope(own_text[...], images_all, offset)[:captions]
    await_far(all_text, 1)
    texts_all = all_text[...].reshape(experts * group, width)
    out_ref[2] = slope(own_image[...], texts_all, offset)[:captions]

    await_bytes(send.at[others], to_expert_s)
    await_bytes(send, fx_s)
    await_bytes(part_send, fc_s)
    await_bytes(part_send, part_s)
    await_bytes(sum_send, sum_s)
    await_bytes(back_send.at[others], back_s)
    for index, (near, every) in enumerate(((near_image, all_image), (near_text, all_text))):
        await_bytes(near.at[pl.ds(1, grids - 1)], near_s.at[index])
        await_bytes(every.at[others], far_s.at[index])


def on_device(
    tokens, routes, route_gates, caption_lengths, image_embed, final_gain, up_weight, down_weight
):
    count, width = tokens.shape
    experts, grids = lax.axis_size("expert"), lax.axis_size("grid")
    slots = 4 * count // experts
    captions = caption_lengths.shape[1]
    group = grids * captions
    inner = up_weight.shape[2]
    dma = pltpu.SemaphoreType.DMA
    whole = pl.BlockSpec(memory_space=pltpu.VMEM)
    far = pl.BlockSpec(memory_space=pl.ANY)
    out = jax.ShapeDtypeStruct((3, captions, width), F32)
    scratch = [
        pltpu.VMEM((width, inner), BF16),
        pltpu.VMEM((width, inner), BF16),
        pltpu.VMEM((inner, width), BF16),
        pltpu.VMEM((experts, slots, width), BF16),
        pltpu.VMEM((count, experts * slots), BF16),
        pltpu.VMEM((count, experts * slots), BF16),
        pltpu.VMEM((experts, grids, slots, width), BF16),
        pltpu.VMEM((experts, 2, slots, width), F32),
        pltpu.VMEM((experts, 2, slots, width), BF16),
        pltpu.VMEM((experts, 2, slots, width), BF16),
    ] + [pltpu.VMEM((experts, slots, width), BF16)] * 4 + [
        pltpu.VMEM((group, width), BF16),
        pltpu.VMEM((grids, group, width), BF16),
        pltpu.VMEM((experts, group, width), BF16),
    ] * 2 + [
        dma((2,)),
        dma, dma((experts,)),
        dma, dma((experts,)),
        dma, dma((experts,)),
        dma, dma((experts,)),
        dma, dma((experts,)),
        dma, dma,
        dma((2,)), dma((2,)), dma((2,)), dma((2,)), dma((2,)), dma((2,)),
    ]
    rows = experts * slots * grids
    result = pl.pallas_call(
        functools.partial(kernel, experts, grids, slots, captions),
        out_shape=out,
        in_specs=[pl.BlockSpec(memory_space=pltpu.SMEM)] + [whole] * 5 + [far] * 2,
        out_specs=whole,
        scratch_shapes=scratch,
        cost_estimate=pl.CostEstimate(
            flops=4 * rows * width * inner, bytes_accessed=4 * width * inner,
            transcendentals=rows * inner,
        ),
        compiler_params=pltpu.CompilerParams(
            collective_id=0, has_side_effects=True, vmem_limit_bytes=56 * 1024 * 1024
        ),
    )(
        caption_lengths, tokens, routes.T, route_gates.T, image_embed, final_gain[None, :],
        up_weight[0], down_weight[0],
    )
    return result[0], result[1], result[2]


def solution(mesh):
    split = P(("expert", "grid"), None)
    return jax.shard_map(
        on_device,
        mesh=mesh,
        in_specs=(split,) * 5 + (P(), P("expert", None, "grid"), P("expert", None, "grid")),
        out_specs=(split,) * 3,
        check_vma=False,
    )
```

```python
import functools
import math

import jax
import jax.numpy as jnp
from jax import lax
from jax.experimental import pallas as pl
from jax.experimental.pallas import tpu as pltpu
from jax.sharding import PartitionSpec as P

EPSILON = 1e-06
SIMILARITY_HEAT = 10.0
MESH = pl.DeviceIdType.MESH
BF16 = jnp.bfloat16
F32 = jnp.float32


def layer_norm(values):
    centred = values - jnp.mean(values, axis=-1, keepdims=True)
    return centred * lax.rsqrt(jnp.mean(centred * centred, axis=-1, keepdims=True) + EPSILON)


def root_norm(values):
    return values * lax.rsqrt(jnp.mean(values * values, axis=-1, keepdims=True) + EPSILON)


def flip(one, other, count):
    total, bit = 0, 1
    while bit < count:
        total = total + bit * (((one // bit) + (other // bit)) % 2)
        bit *= 2
    return total


def halves(values):
    high = values.astype(BF16)
    return high, (values - high.astype(F32)).astype(BF16)


def dot(left, right):
    return jnp.dot(left, right, preferred_element_type=F32)


def dot_nt(left, right):
    return lax.dot_general(left, right, (((1,), (1,)), ((), ())), preferred_element_type=F32)


def join(values, rows):
    width = values.shape[-1]
    if values.shape[-2] % 16 == 0:
        return values.reshape(rows, width)
    return values.astype(F32).reshape(rows, width).astype(values.dtype)


def part(values, lead):
    return values.reshape(lead + (values.shape[0] // math.prod(lead), values.shape[-1]))


def gelu(values):
    size = jnp.abs(values)
    t = 1.0 / (1.0 + (0.3275911 * math.sqrt(0.5)) * size)
    series = 0.5 * 1.061405429
    for term in (-1.453152027, 1.421413741, -0.284496736, 0.254829592):
        series = series * t + 0.5 * term
    tail = series * t * jnp.exp(values * values * -0.5)
    return jnp.maximum(values, 0.0) - size * tail


def slope(own, every, offset):
    logits = SIMILARITY_HEAT * dot_nt(own, every)
    row = lax.broadcasted_iota(jnp.int32, logits.shape, 0)
    column = lax.broadcasted_iota(jnp.int32, logits.shape, 1)
    signs = jnp.where(column == row + offset, 1.0, -1.0).astype(F32)
    coeff = -signs * jax.nn.sigmoid(-signs * logits)
    high, low = halves(coeff)
    return SIMILARITY_HEAT * (dot(high, every) + dot(low, every))


def kernel(
    experts, grids, slots, captions,
    lengths_ref, tokens_ref, routes_ref, gates_ref, image_ref, gain_ref, up_hbm, down_hbm,
    out_ref,
    up_ref, down_ref, down_turned, send, gate_high, gate_low, rows, own, part_send, part_in, sum_send, sum_in,
    back_send, back_in, own_image, near_image, all_image, own_text, near_text, all_text,
    weight_sem, to_expert_s, to_expert_r, fx_s, fx_r, fc_s, fc_r, part_s, part_r, sum_s, sum_r,
    back_s, back_r, near_s, near_r, far_s, far_r, across_r, spread_r,
):
    e = lax.axis_index("expert")
    g = lax.axis_index("grid")
    core = (e, g + 1 - 2 * (g % 2))
    cross = (e, (g + grids // 2) % grids)
    tokens, width = tokens_ref.shape
    group = grids * captions

    half = experts // 2

    def order(position):
        turned = position + experts - 1
        turn_of = turned % experts
        pair, odd = turn_of // 2 + 1, turn_of % 2
        return (turned // experts) * ((1 - odd) * pair + odd * (half + pair % half))

    opposite = ((e + half) % experts, g)

    def near_peer(step):
        return (flip(e, step, experts), g)

    def expert_peer(step):
        return (flip(e, order(step), experts), g)

    def push(source, target, send_sem, recv_sem, device):
        pltpu.make_async_remote_copy(
            src_ref=source, dst_ref=target, send_sem=send_sem, recv_sem=recv_sem,
            device_id=device, device_id_type=MESH,
        ).start()

    def await_bytes(ref, sem):
        pltpu.make_async_copy(ref, ref, sem).wait()

    barrier = pltpu.get_barrier_semaphore()

    def greet(step, carry):
        pl.semaphore_signal(barrier, inc=1, device_id=expert_peer(step), device_id_type=MESH)
        return carry

    lax.fori_loop(1, experts, greet, 0)
    for hop in range(1, grids):
        pl.semaphore_signal(barrier, inc=1, device_id=(e, (g + hop) % grids), device_id_type=MESH)
    load_up = pltpu.make_async_copy(up_hbm, up_ref, weight_sem.at[0])
    load_up.start()
    load_down = pltpu.make_async_copy(down_hbm, down_ref, weight_sem.at[1])
    load_down.start()

    normed = layer_norm(tokens_ref[...].astype(F32)).astype(BF16)
    routes = routes_ref[...]
    first, second = routes[0:1, :], routes[1:2, :]
    ids = lax.broadcasted_iota(jnp.int32, (max(experts, 8), tokens), 0)
    named = ((ids == first) | (ids == second)).astype(F32).astype(BF16)
    before = lax.broadcasted_iota(jnp.int32, (tokens, tokens), 0)
    after = lax.broadcasted_iota(jnp.int32, (tokens, tokens), 1)
    ranks = dot(named, (before < after).astype(F32).astype(BF16))
    spots = lax.broadcasted_iota(jnp.int32, (experts * slots, tokens), 0)
    hits = []
    for chosen in (first, second):
        rank = jnp.sum(jnp.where(ids == chosen, ranks, 0.0), axis=0, keepdims=True)
        far = flip(chosen, e, experts)
        spot_of = jnp.where(far > half, 2 * (far - half), jnp.maximum(2 * far - 1, 0))
        hits.append(spots == spot_of * slots + rank.astype(jnp.int32))
    taken = (hits[0] | hits[1]).astype(F32).astype(BF16)
    blocks = part(dot(taken, normed), (experts,)).astype(BF16)
    send[...] = blocks
    rows[0, 0] = blocks[0]
    pl.semaphore_wait(barrier, experts + grids - 2)

    def dispatch(step, carry):
        push(send.at[step], rows.at[step, 0], to_expert_s, to_expert_r.at[step], expert_peer(step))
        return carry

    ahead = min(4, experts)
    lax.fori_loop(1, ahead, dispatch, 0)
    push(rows.at[0, 0], rows.at[0, 1], fx_s, fx_r.at[0], cross)
    push(rows.at[0, 0], rows.at[0, 2], fc_s, fc_r.at[0], core)
    weights = jnp.where(hits[0], gates_ref[0:1, :], 0.0) + jnp.where(hits[1], gates_ref[1:2, :], 0.0)
    high, low = halves(weights.T)
    gate_high[...] = high
    gate_low[...] = low

    line = lax.broadcasted_iota(jnp.int32, (2 * group, 1), 0)
    caption = jnp.where(line < group, line - g * captions, line - group)
    images = root_norm(image_ref[...].astype(F32)) / math.sqrt(width)
    spread = jnp.zeros((2 * group, width), F32)
    for index in range(captions):
        spread = jnp.where(caption == index, images[index:index + 1, :], spread)
    near_image[0] = spread[:group].astype(BF16)
    own_image[...] = spread[group:].astype(BF16)

    def share_near(near, index):
        for hop in range(1, grids):
            push(near.at[0], near.at[hop], near_s.at[index], near_r.at[index], (e, (g + hop) % grids))

    def share_far(near, every, index):
        await_bytes(near.at[pl.ds(1, grids - 1)], near_r.at[index])
        total = near[0].astype(F32)
        for hop in range(1, grids):
            total = total + near[hop].astype(F32)
        every[0] = total.astype(BF16)

        push(every.at[0], every.at[half], far_s.at[index], across_r.at[index], opposite)

        def each(step, carry):
            push(every.at[0], every.at[step], far_s.at[index], far_r.at[index], near_peer(step))
            return carry

        lax.fori_loop(1, half, each, 0)

    def spread_far(every, index):
        await_bytes(every.at[half], across_r.at[index])

        def each(step, carry):
            push(
                every.at[half], every.at[half + step], far_s.at[index], spread_r.at[index],
                near_peer(step),
            )
            return carry

        lax.fori_loop(1, half, each, 0)

    def await_far(every, index):
        await_bytes(every.at[pl.ds(1, half - 1)], far_r.at[index])
        await_bytes(every.at[pl.ds(half + 1, half - 1)], spread_r.at[index])

    share_near(near_image, 0)

    tile = up_ref.shape[1] // 4

    def turn(index, carry):
        @pl.when(index + ahead < experts)
        def _():
            dispatch(index + ahead, 0)

        @pl.when((index > 0) & (index < experts))
        def _():
            at = index
            await_bytes(rows.at[at, 0], to_expert_r.at[at])
            push(rows.at[at, 0], rows.at[at, 1], fx_s, fx_r.at[at], cross)
            push(rows.at[at, 0], rows.at[at, 2], fc_s, fc_r.at[at], core)

        @pl.when((index >= 2) & (index < experts + 2))
        def _():
            at = index - 2
            await_bytes(rows.at[at, 1], fx_r.at[at])
            push(rows.at[at, 1], rows.at[at, 3], fc_s, fc_r.at[at], core)

        @pl.when(index == 1)
        def _():
            share_far(near_image, all_image, 0)
            load_up.wait()
            load_down.wait()
            for low in range(0, 4 * tile, tile):
                down_turned[low:low + tile] = down_ref[:, low:low + tile].T

        @pl.when((index >= 3) & (index < experts + 3))
        def _():
            at = index - 3
            await_bytes(rows.at[at, pl.ds(2, 2)], fc_r.at[at])
            block = join(rows[at], grids * slots)
            parts = [
                gelu(dot(block, up_ref[:, low:low + tile])).astype(BF16)
                for low in range(0, 4 * tile, tile)
            ]
            term = part(dot(jnp.concatenate(parts, axis=1), down_turned[...]), (grids,))
            own[at] = term[:2]
            part_send[at] = term[2:].astype(BF16)
            push(part_send.at[at], part_in.at[at], part_s, part_r.at[at], core)

        @pl.when(index == 3)
        def _():
            spread_far(all_image, 0)

        @pl.when((index >= 4) & (index < experts + 4))
        def _():
            at = index - 4
            await_bytes(part_in.at[at], part_r.at[at])
            sum_send[at] = (own[at, 1] + part_in[at, 1].astype(F32)).astype(BF16)
            push(sum_send.at[at], sum_in.at[at], sum_s, sum_r.at[at], cross)

        @pl.when(index >= 6)
        def _():
            at = index - 6
            await_bytes(sum_in.at[at], sum_r.at[at])
            result = own[at, 0] + part_in[at, 0].astype(F32) + sum_in[at].astype(F32)

            @pl.when(at == 0)
            def _():
                back_in[0] = result.astype(BF16)

            @pl.when(at > 0)
            def _():
                back_send[at] = result.astype(BF16)
                push(back_send.at[at], back_in.at[at], back_s, back_r, expert_peer(at))

        return carry

    lax.fori_loop(0, experts + 6, turn, 0)

    await_bytes(back_in.at[pl.ds(1, experts - 1)], back_r)
    returned = join(back_in[...], experts * slots)
    picked = dot(gate_high[...], returned) + dot(gate_low[...], returned)
    final = layer_norm(tokens_ref[...].astype(F32) + picked) * gain_ref[...]
    starts = jnp.zeros((2 * group, 1), jnp.int32)
    ends = jnp.zeros((2 * group, 1), jnp.int32)
    reached = 0
    for index in range(captions):
        starts = jnp.where(caption == index, reached, starts)
        reached = reached + lengths_ref[0, index]
        ends = jnp.where(caption == index, reached, ends)
    spot = lax.broadcasted_iota(jnp.int32, (2 * group, tokens), 1)
    members = ((spot >= starts) & (spot < ends)).astype(F32).astype(BF16)
    high, low = halves(final)
    pooled = (dot(members, high) + dot(members, low)) / jnp.maximum(ends - starts, 1).astype(F32)
    embed = root_norm(pooled)
    out_ref[0] = embed[group:group + captions]
    direction = embed / math.sqrt(width)
    near_text[0] = direction[:group].astype(BF16)
    own_text[...] = direction[group:].astype(BF16)
    share_near(near_text, 1)
    share_far(near_text, all_text, 1)

    others = pl.ds(1, experts - 1)
    spread_far(all_text, 1)
    await_far(all_image, 0)
    images_all = all_image[...].reshape(experts * group, width)
    offset = g * captions
    out_ref[1] = slope(own_text[...], images_all, offset)[:captions]
    await_far(all_text, 1)
    texts_all = all_text[...].reshape(experts * group, width)
    out_ref[2] = slope(own_image[...], texts_all, offset)[:captions]

    await_bytes(send.at[others], to_expert_s)
    await_bytes(send, fx_s)
    await_bytes(part_send, fc_s)
    await_bytes(part_send, part_s)
    await_bytes(sum_send, sum_s)
    await_bytes(back_send.at[others], back_s)
    for index, (near, every) in enumerate(((near_image, all_image), (near_text, all_text))):
        await_bytes(near.at[pl.ds(1, grids - 1)], near_s.at[index])
        await_bytes(every.at[others], far_s.at[index])


def on_device(
    tokens, routes, route_gates, caption_lengths, image_embed, final_gain, up_weight, down_weight
):
    count, width = tokens.shape
    experts, grids = lax.axis_size("expert"), lax.axis_size("grid")
    slots = 4 * count // experts
    captions = caption_lengths.shape[1]
    group = grids * captions
    inner = up_weight.shape[2]
    dma = pltpu.SemaphoreType.DMA
    whole = pl.BlockSpec(memory_space=pltpu.VMEM)
    far = pl.BlockSpec(memory_space=pl.ANY)
    out = jax.ShapeDtypeStruct((3, captions, width), F32)
    scratch = [
        pltpu.VMEM((width, inner), BF16),
        pltpu.VMEM((width, inner), BF16),
        pltpu.VMEM((inner, width), BF16),
        pltpu.VMEM((experts, slots, width), BF16),
        pltpu.VMEM((count, experts * slots), BF16),
        pltpu.VMEM((count, experts * slots), BF16),
        pltpu.VMEM((experts, grids, slots, width), BF16),
        pltpu.VMEM((experts, 2, slots, width), F32),
        pltpu.VMEM((experts, 2, slots, width), BF16),
        pltpu.VMEM((experts, 2, slots, width), BF16),
    ] + [pltpu.VMEM((experts, slots, width), BF16)] * 4 + [
        pltpu.VMEM((group, width), BF16),
        pltpu.VMEM((grids, group, width), BF16),
        pltpu.VMEM((experts, group, width), BF16),
    ] * 2 + [
        dma((2,)),
        dma, dma((experts,)),
        dma, dma((experts,)),
        dma, dma((experts,)),
        dma, dma((experts,)),
        dma, dma((experts,)),
        dma, dma,
        dma((2,)), dma((2,)), dma((2,)), dma((2,)), dma((2,)), dma((2,)),
    ]
    rows = experts * slots * grids
    result = pl.pallas_call(
        functools.partial(kernel, experts, grids, slots, captions),
        out_shape=out,
        in_specs=[pl.BlockSpec(memory_space=pltpu.SMEM)] + [whole] * 5 + [far] * 2,
        out_specs=whole,
        scratch_shapes=scratch,
        cost_estimate=pl.CostEstimate(
            flops=4 * rows * width * inner, bytes_accessed=4 * width * inner,
            transcendentals=rows * inner,
        ),
        compiler_params=pltpu.CompilerParams(
            collective_id=0, has_side_effects=True, vmem_limit_bytes=56 * 1024 * 1024
        ),
    )(
        caption_lengths, tokens, routes.T, route_gates.T, image_embed, final_gain[None, :],
        up_weight[0], down_weight[0],
    )
    return result[0], result[1], result[2]


def solution(mesh):
    split = P(("expert", "grid"), None)
    return jax.shard_map(
        on_device,
        mesh=mesh,
        in_specs=(split,) * 5 + (P(), P("expert", None, "grid"), P("expert", None, "grid")),
        out_specs=(split,) * 3,
        check_vma=False,
    )
```

```python
import functools
import math

import jax
import jax.numpy as jnp
from jax import lax
from jax.experimental import pallas as pl
from jax.experimental.pallas import tpu as pltpu
from jax.sharding import PartitionSpec as P

EPSILON = 1e-06
SIMILARITY_HEAT = 10.0
MESH = pl.DeviceIdType.MESH
BF16 = jnp.bfloat16
F32 = jnp.float32


def layer_norm(values):
    centred = values - jnp.mean(values, axis=-1, keepdims=True)
    return centred * lax.rsqrt(jnp.mean(centred * centred, axis=-1, keepdims=True) + EPSILON)


def root_norm(values):
    return values * lax.rsqrt(jnp.mean(values * values, axis=-1, keepdims=True) + EPSILON)


def flip(one, other, count):
    total, bit = 0, 1
    while bit < count:
        total = total + bit * (((one // bit) + (other // bit)) % 2)
        bit *= 2
    return total


def halves(values):
    high = values.astype(BF16)
    return high, (values - high.astype(F32)).astype(BF16)


def dot(left, right):
    return jnp.dot(left, right, preferred_element_type=F32)


def dot_nt(left, right):
    return lax.dot_general(left, right, (((1,), (1,)), ((), ())), preferred_element_type=F32)


def join(values, rows):
    width = values.shape[-1]
    if values.shape[-2] % 16 == 0:
        return values.reshape(rows, width)
    return values.astype(F32).reshape(rows, width).astype(values.dtype)


def part(values, lead):
    return values.reshape(lead + (values.shape[0] // math.prod(lead), values.shape[-1]))


def gelu(values):
    size = jnp.abs(values)
    t = 1.0 / (1.0 + (0.3275911 * math.sqrt(0.5)) * size)
    series = 0.5 * 1.061405429
    for term in (-1.453152027, 1.421413741, -0.284496736, 0.254829592):
        series = series * t + 0.5 * term
    tail = series * t * jnp.exp(values * values * -0.5)
    return jnp.maximum(values, 0.0) - size * tail


def slope(own, every, offset):
    logits = SIMILARITY_HEAT * dot_nt(own, every)
    row = lax.broadcasted_iota(jnp.int32, logits.shape, 0)
    column = lax.broadcasted_iota(jnp.int32, logits.shape, 1)
    signs = jnp.where(column == row + offset, 1.0, -1.0).astype(F32)
    coeff = -signs * jax.nn.sigmoid(-signs * logits)
    high, low = halves(coeff)
    return SIMILARITY_HEAT * (dot(high, every) + dot(low, every))


def kernel(
    experts, grids, slots, captions,
    lengths_ref, tokens_ref, routes_ref, gates_ref, image_ref, gain_ref, up_hbm, down_hbm,
    out_ref,
    up_ref, down_ref, send, gate_high, gate_low, rows, own, sum_send, sum_in,
    back_send, back_in, own_image, near_image, all_image, own_text, near_text, all_text,
    weight_sem, to_expert_s, to_expert_r, fx_s, fx_r, core_s, core_r, sum_s, sum_r,
    back_s, back_r, near_s, near_r, far_s, far_r, across_r, spread_r,
):
    e = lax.axis_index("expert")
    g = lax.axis_index("grid")
    core = (e, g + 1 - 2 * (g % 2))
    cross = (e, (g + grids // 2) % grids)
    tokens, width = tokens_ref.shape
    group = grids * captions

    half = experts // 2

    def order(position):
        turned = position + experts - 1
        turn_of = turned % experts
        pair, odd = turn_of // 2 + 1, turn_of % 2
        return (turned // experts) * ((1 - odd) * pair + odd * (half + pair % half))

    opposite = ((e + half) % experts, g)

    def near_peer(step):
        return (flip(e, step, experts), g)

    def expert_peer(step):
        return (flip(e, order(step), experts), g)

    def push(source, target, send_sem, recv_sem, device):
        pltpu.make_async_remote_copy(
            src_ref=source, dst_ref=target, send_sem=send_sem, recv_sem=recv_sem,
            device_id=device, device_id_type=MESH,
        ).start()

    def await_bytes(ref, sem):
        pltpu.make_async_copy(ref, ref, sem).wait()

    barrier = pltpu.get_barrier_semaphore()

    def greet(step, carry):
        pl.semaphore_signal(barrier, inc=1, device_id=expert_peer(step), device_id_type=MESH)
        return carry

    lax.fori_loop(1, experts, greet, 0)
    for hop in range(1, grids):
        pl.semaphore_signal(barrier, inc=1, device_id=(e, (g + hop) % grids), device_id_type=MESH)
    load_up = pltpu.make_async_copy(up_hbm, up_ref.at[0], weight_sem.at[0])
    load_up.start()
    load_down = pltpu.make_async_copy(down_hbm, down_ref.at[0], weight_sem.at[1])
    load_down.start()

    normed = layer_norm(tokens_ref[...].astype(F32)).astype(BF16)
    routes = routes_ref[...]
    first, second = routes[0:1, :], routes[1:2, :]
    ids = lax.broadcasted_iota(jnp.int32, (max(experts, 8), tokens), 0)
    named = ((ids == first) | (ids == second)).astype(F32).astype(BF16)
    before = lax.broadcasted_iota(jnp.int32, (tokens, tokens), 0)
    after = lax.broadcasted_iota(jnp.int32, (tokens, tokens), 1)
    ranks = dot(named, (before < after).astype(F32).astype(BF16))
    spots = lax.broadcasted_iota(jnp.int32, (experts * slots, tokens), 0)
    hits = []
    for chosen in (first, second):
        rank = jnp.sum(jnp.where(ids == chosen, ranks, 0.0), axis=0, keepdims=True)
        far = flip(chosen, e, experts)
        spot_of = jnp.where(far > half, 2 * (far - half), jnp.maximum(2 * far - 1, 0))
        hits.append(spots == spot_of * slots + rank.astype(jnp.int32))
    taken = (hits[0] | hits[1]).astype(F32).astype(BF16)
    blocks = part(dot(taken, normed), (experts,)).astype(BF16)
    send[...] = blocks
    rows[0, 0] = blocks[0]
    pl.semaphore_wait(barrier, experts + grids - 2)

    def dispatch(step, carry):
        push(send.at[step], rows.at[step, 0], to_expert_s, to_expert_r.at[step], expert_peer(step))
        return carry

    ahead = min(4, experts)
    lax.fori_loop(1, ahead, dispatch, 0)
    push(rows.at[0, 0], rows.at[0, 1], fx_s, fx_r.at[0], cross)
    push(up_hbm, up_ref.at[1], core_s.at[0], core_r.at[0], core)
    push(down_hbm, down_ref.at[1], core_s.at[1], core_r.at[1], core)
    weights = jnp.where(hits[0], gates_ref[0:1, :], 0.0) + jnp.where(hits[1], gates_ref[1:2, :], 0.0)
    high, low = halves(weights.T)
    gate_high[...] = high
    gate_low[...] = low

    line = lax.broadcasted_iota(jnp.int32, (2 * group, 1), 0)
    caption = jnp.where(line < group, line - g * captions, line - group)
    images = root_norm(image_ref[...].astype(F32)) / math.sqrt(width)
    spread = jnp.zeros((2 * group, width), F32)
    for index in range(captions):
        spread = jnp.where(caption == index, images[index:index + 1, :], spread)
    near_image[0] = spread[:group].astype(BF16)
    own_image[...] = spread[group:].astype(BF16)

    def share_near(near, index):
        for hop in range(1, grids):
            push(near.at[0], near.at[hop], near_s.at[index], near_r.at[index], (e, (g + hop) % grids))

    def share_far(near, every, index):
        await_bytes(near.at[pl.ds(1, grids - 1)], near_r.at[index])
        total = near[0].astype(F32)
        for hop in range(1, grids):
            total = total + near[hop].astype(F32)
        every[0] = total.astype(BF16)

        push(every.at[0], every.at[half], far_s.at[index], across_r.at[index], opposite)

        def each(step, carry):
            push(every.at[0], every.at[step], far_s.at[index], far_r.at[index], near_peer(step))
            return carry

        lax.fori_loop(1, half, each, 0)

    def spread_far(every, index):
        await_bytes(every.at[half], across_r.at[index])

        def each(step, carry):
            push(
                every.at[half], every.at[half + step], far_s.at[index], spread_r.at[index],
                near_peer(step),
            )
            return carry

        lax.fori_loop(1, half, each, 0)

    def await_far(every, index):
        await_bytes(every.at[pl.ds(1, half - 1)], far_r.at[index])
        await_bytes(every.at[pl.ds(half + 1, half - 1)], spread_r.at[index])

    share_near(near_image, 0)

    tile = up_ref.shape[2] // 4

    def turn(index, carry):
        @pl.when(index + ahead < experts)
        def _():
            dispatch(index + ahead, 0)

        @pl.when((index > 0) & (index < experts))
        def _():
            at = index
            await_bytes(rows.at[at, 0], to_expert_r.at[at])
            push(rows.at[at, 0], rows.at[at, 1], fx_s, fx_r.at[at], cross)

        @pl.when(index == 1)
        def _():
            share_far(near_image, all_image, 0)
            load_up.wait()
            load_down.wait()

        @pl.when(index == 2)
        def _():
            await_bytes(up_ref.at[1], core_r.at[0])
            await_bytes(down_ref.at[1], core_r.at[1])

        @pl.when((index >= 3) & (index < experts + 3) & (index % 2 == 1))
        def _():
            at = index - 3
            both = pl.ds(at, 2)
            for later in range(2):
                await_bytes(rows.at[at + later, 1], fx_r.at[at + later])
            block = join(rows[both], 4 * slots)
            term = None
            for side in range(2):
                parts = [
                    gelu(dot(block, up_ref[side, :, low:low + tile])).astype(BF16)
                    for low in range(0, 4 * tile, tile)
                ]
                product = dot_nt(jnp.concatenate(parts, axis=1), down_ref[side])
                term = product if term is None else term + product
            term = part(term, (2, 2))
            own[both] = term[:, 0]
            sum_send[both] = term[:, 1].astype(BF16)
            for later in range(2):
                push(
                    sum_send.at[at + later], sum_in.at[at + later], sum_s, sum_r.at[at + later],
                    cross,
                )

        @pl.when(index == 3)
        def _():
            spread_far(all_image, 0)

        @pl.when(index >= 5)
        def _():
            at = index - 5
            await_bytes(sum_in.at[at], sum_r.at[at])
            result = own[at] + sum_in[at].astype(F32)

            @pl.when(at == 0)
            def _():
                back_in[0] = result.astype(BF16)

            @pl.when(at > 0)
            def _():
                back_send[at] = result.astype(BF16)
                push(back_send.at[at], back_in.at[at], back_s, back_r, expert_peer(at))

        return carry

    lax.fori_loop(0, experts + 5, turn, 0)

    await_bytes(back_in.at[pl.ds(1, experts - 1)], back_r)
    returned = join(back_in[...], experts * slots)
    picked = dot(gate_high[...], returned) + dot(gate_low[...], returned)
    final = layer_norm(tokens_ref[...].astype(F32) + picked) * gain_ref[...]
    starts = jnp.zeros((2 * group, 1), jnp.int32)
    ends = jnp.zeros((2 * group, 1), jnp.int32)
    reached = 0
    for index in range(captions):
        starts = jnp.where(caption == index, reached, starts)
        reached = reached + lengths_ref[0, index]
        ends = jnp.where(caption == index, reached, ends)
    spot = lax.broadcasted_iota(jnp.int32, (2 * group, tokens), 1)
    members = ((spot >= starts) & (spot < ends)).astype(F32).astype(BF16)
    high, low = halves(final)
    pooled = (dot(members, high) + dot(members, low)) / jnp.maximum(ends - starts, 1).astype(F32)
    embed = root_norm(pooled)
    out_ref[0] = embed[group:group + captions]
    direction = embed / math.sqrt(width)
    near_text[0] = direction[:group].astype(BF16)
    own_text[...] = direction[group:].astype(BF16)
    share_near(near_text, 1)
    share_far(near_text, all_text, 1)

    others = pl.ds(1, experts - 1)
    spread_far(all_text, 1)
    await_far(all_image, 0)
    images_all = all_image[...].reshape(experts * group, width)
    offset = g * captions
    out_ref[1] = slope(own_text[...], images_all, offset)[:captions]
    await_far(all_text, 1)
    texts_all = all_text[...].reshape(experts * group, width)
    out_ref[2] = slope(own_image[...], texts_all, offset)[:captions]

    await_bytes(send.at[others], to_expert_s)
    await_bytes(send, fx_s)
    await_bytes(up_ref.at[1], core_s.at[0])
    await_bytes(down_ref.at[1], core_s.at[1])
    await_bytes(sum_send, sum_s)
    await_bytes(back_send.at[others], back_s)
    for index, (near, every) in enumerate(((near_image, all_image), (near_text, all_text))):
        await_bytes(near.at[pl.ds(1, grids - 1)], near_s.at[index])
        await_bytes(every.at[others], far_s.at[index])


def on_device(
    tokens, routes, route_gates, caption_lengths, image_embed, final_gain, up_weight, down_weight
):
    count, width = tokens.shape
    experts, grids = lax.axis_size("expert"), lax.axis_size("grid")
    slots = 4 * count // experts
    captions = caption_lengths.shape[1]
    group = grids * captions
    inner = up_weight.shape[2]
    dma = pltpu.SemaphoreType.DMA
    whole = pl.BlockSpec(memory_space=pltpu.VMEM)
    far = pl.BlockSpec(memory_space=pl.ANY)
    out = jax.ShapeDtypeStruct((3, captions, width), F32)
    scratch = [
        pltpu.VMEM((2, width, inner), BF16),
        pltpu.VMEM((2, width, inner), BF16),
        pltpu.VMEM((experts, slots, width), BF16),
        pltpu.VMEM((count, experts * slots), BF16),
        pltpu.VMEM((count, experts * slots), BF16),
        pltpu.VMEM((experts, 2, slots, width), BF16),
        pltpu.VMEM((experts, slots, width), F32),
    ] + [pltpu.VMEM((experts, slots, width), BF16)] * 4 + [
        pltpu.VMEM((group, width), BF16),
        pltpu.VMEM((grids, group, width), BF16),
        pltpu.VMEM((experts, group, width), BF16),
    ] * 2 + [
        dma((2,)),
        dma, dma((experts,)),
        dma, dma((experts,)),
        dma((2,)), dma((2,)),
        dma, dma((experts,)),
        dma, dma,
        dma((2,)), dma((2,)), dma((2,)), dma((2,)), dma((2,)), dma((2,)),
    ]
    rows = experts * slots * grids
    result = pl.pallas_call(
        functools.partial(kernel, experts, grids, slots, captions),
        out_shape=out,
        in_specs=[pl.BlockSpec(memory_space=pltpu.SMEM)] + [whole] * 5 + [far] * 2,
        out_specs=whole,
        scratch_shapes=scratch,
        cost_estimate=pl.CostEstimate(
            flops=4 * rows * width * inner, bytes_accessed=4 * width * inner,
            transcendentals=rows * inner,
        ),
        compiler_params=pltpu.CompilerParams(
            collective_id=0, has_side_effects=True, vmem_limit_bytes=56 * 1024 * 1024
        ),
    )(
        caption_lengths, tokens, routes.T, route_gates.T, image_embed, final_gain[None, :],
        up_weight[0], down_weight[0],
    )
    return result[0], result[1], result[2]


def solution(mesh):
    split = P(("expert", "grid"), None)
    return jax.shard_map(
        on_device,
        mesh=mesh,
        in_specs=(split,) * 5 + (P(), P("expert", None, "grid"), P("expert", None, "grid")),
        out_specs=(split,) * 3,
        check_vma=False,
    )
```

```python
import functools
import math

import jax
import jax.numpy as jnp
from jax import lax
from jax.experimental import pallas as pl
from jax.experimental.pallas import tpu as pltpu
from jax.sharding import PartitionSpec as P

EPSILON = 1e-06
SIMILARITY_HEAT = 10.0
MESH = pl.DeviceIdType.MESH
BF16 = jnp.bfloat16
F32 = jnp.float32


def layer_norm(values):
    centred = values - jnp.mean(values, axis=-1, keepdims=True)
    return centred * lax.rsqrt(jnp.mean(centred * centred, axis=-1, keepdims=True) + EPSILON)


def root_norm(values):
    return values * lax.rsqrt(jnp.mean(values * values, axis=-1, keepdims=True) + EPSILON)


def flip(one, other, count):
    total, bit = 0, 1
    while bit < count:
        total = total + bit * (((one // bit) + (other // bit)) % 2)
        bit *= 2
    return total


def halves(values):
    high = values.astype(BF16)
    return high, (values - high.astype(F32)).astype(BF16)


def dot(left, right):
    return jnp.dot(left, right, preferred_element_type=F32)


def dot_nt(left, right):
    return lax.dot_general(left, right, (((1,), (1,)), ((), ())), preferred_element_type=F32)


def join(values, rows):
    width = values.shape[-1]
    if values.shape[-2] % 16 == 0:
        return values.reshape(rows, width)
    return values.astype(F32).reshape(rows, width).astype(values.dtype)


def part(values, lead):
    return values.reshape(lead + (values.shape[0] // math.prod(lead), values.shape[-1]))


def gelu(values):
    size = jnp.abs(values)
    t = 1.0 / (1.0 + (0.3275911 * math.sqrt(0.5)) * size)
    series = 0.5 * 1.061405429
    for term in (-1.453152027, 1.421413741, -0.284496736, 0.254829592):
        series = series * t + 0.5 * term
    tail = series * t * jnp.exp(values * values * -0.5)
    return jnp.maximum(values, 0.0) - size * tail


def slope(own, every, offset):
    logits = SIMILARITY_HEAT * dot_nt(own, every)
    row = lax.broadcasted_iota(jnp.int32, logits.shape, 0)
    column = lax.broadcasted_iota(jnp.int32, logits.shape, 1)
    signs = jnp.where(column == row + offset, 1.0, -1.0).astype(F32)
    coeff = -signs * jax.nn.sigmoid(-signs * logits)
    high, low = halves(coeff)
    return SIMILARITY_HEAT * (dot(high, every) + dot(low, every))


def kernel(
    experts, grids, slots, captions,
    lengths_ref, tokens_ref, routes_ref, gates_ref, image_ref, gain_ref, up_hbm, down_hbm,
    out_ref,
    up_ref, down_ref, send, gate_high, gate_low, rows, own, sum_send, sum_in,
    back_send, back_in, own_image, near_image, all_image, own_text, near_text, all_text,
    weight_sem, to_expert_s, to_expert_r, fx_s, fx_r, core_s, core_r, sum_s, sum_r,
    back_s, back_r, near_s, near_r, far_s, far_r, across_r, spread_r,
):
    e = lax.axis_index("expert")
    g = lax.axis_index("grid")
    core = (e, g + 1 - 2 * (g % 2))
    cross = (e, (g + grids // 2) % grids)
    tokens, width = tokens_ref.shape
    group = grids * captions

    half = experts // 2

    def order(position):
        turned = position + experts - 1
        turn_of = turned % experts
        pair, odd = turn_of // 2 + 1, turn_of % 2
        return (turned // experts) * ((1 - odd) * pair + odd * (half + pair % half))

    opposite = ((e + half) % experts, g)

    def near_peer(step):
        return (flip(e, step, experts), g)

    def expert_peer(step):
        return (flip(e, order(step), experts), g)

    def push(source, target, send_sem, recv_sem, device):
        pltpu.make_async_remote_copy(
            src_ref=source, dst_ref=target, send_sem=send_sem, recv_sem=recv_sem,
            device_id=device, device_id_type=MESH,
        ).start()

    def await_bytes(ref, sem):
        pltpu.make_async_copy(ref, ref, sem).wait()

    barrier = pltpu.get_barrier_semaphore()

    def greet(step, carry):
        pl.semaphore_signal(barrier, inc=1, device_id=expert_peer(step), device_id_type=MESH)
        return carry

    lax.fori_loop(1, experts, greet, 0)
    for hop in range(1, grids):
        pl.semaphore_signal(barrier, inc=1, device_id=(e, (g + hop) % grids), device_id_type=MESH)
    pl.semaphore_wait(barrier, experts + grids - 2)
    push(up_hbm, up_ref.at[1], core_s.at[0], core_r.at[0], core)
    push(down_hbm, down_ref.at[1], core_s.at[1], core_r.at[1], core)
    load_up = pltpu.make_async_copy(up_hbm, up_ref.at[0], weight_sem.at[0])
    load_up.start()
    load_down = pltpu.make_async_copy(down_hbm, down_ref.at[0], weight_sem.at[1])
    load_down.start()

    normed = layer_norm(tokens_ref[...].astype(F32)).astype(BF16)
    routes = routes_ref[...]
    first, second = routes[0:1, :], routes[1:2, :]
    ids = lax.broadcasted_iota(jnp.int32, (max(experts, 8), tokens), 0)
    named = ((ids == first) | (ids == second)).astype(F32).astype(BF16)
    before = lax.broadcasted_iota(jnp.int32, (tokens, tokens), 0)
    after = lax.broadcasted_iota(jnp.int32, (tokens, tokens), 1)
    ranks = dot(named, (before < after).astype(F32).astype(BF16))
    spots = lax.broadcasted_iota(jnp.int32, (experts * slots, tokens), 0)
    hits = []
    for chosen in (first, second):
        rank = jnp.sum(jnp.where(ids == chosen, ranks, 0.0), axis=0, keepdims=True)
        far = flip(chosen, e, experts)
        spot_of = jnp.where(far > half, 2 * (far - half), jnp.maximum(2 * far - 1, 0))
        hits.append(spots == spot_of * slots + rank.astype(jnp.int32))
    taken = (hits[0] | hits[1]).astype(F32).astype(BF16)
    blocks = part(dot(taken, normed), (experts,)).astype(BF16)
    send[...] = blocks
    rows[0, 0] = blocks[0]

    def dispatch(step, carry):
        push(send.at[step], rows.at[step, 0], to_expert_s, to_expert_r.at[step], expert_peer(step))
        return carry

    ahead = min(4, experts)
    lax.fori_loop(1, ahead, dispatch, 0)
    push(rows.at[0, 0], rows.at[0, 1], fx_s, fx_r.at[0], cross)
    weights = jnp.where(hits[0], gates_ref[0:1, :], 0.0) + jnp.where(hits[1], gates_ref[1:2, :], 0.0)
    high, low = halves(weights.T)
    gate_high[...] = high
    gate_low[...] = low

    line = lax.broadcasted_iota(jnp.int32, (2 * group, 1), 0)
    caption = jnp.where(line < group, line - g * captions, line - group)
    images = root_norm(image_ref[...].astype(F32)) / math.sqrt(width)
    spread = jnp.zeros((2 * group, width), F32)
    for index in range(captions):
        spread = jnp.where(caption == index, images[index:index + 1, :], spread)
    near_image[0] = spread[:group].astype(BF16)
    own_image[...] = spread[group:].astype(BF16)

    def share_near(near, index):
        for hop in range(1, grids):
            push(near.at[0], near.at[hop], near_s.at[index], near_r.at[index], (e, (g + hop) % grids))

    def share_far(near, every, index):
        await_bytes(near.at[pl.ds(1, grids - 1)], near_r.at[index])
        total = near[0].astype(F32)
        for hop in range(1, grids):
            total = total + near[hop].astype(F32)
        every[0] = total.astype(BF16)

        push(every.at[0], every.at[half], far_s.at[index], across_r.at[index], opposite)

        def each(step, carry):
            push(every.at[0], every.at[step], far_s.at[index], far_r.at[index], near_peer(step))
            return carry

        lax.fori_loop(1, half, each, 0)

    def spread_far(every, index):
        await_bytes(every.at[half], across_r.at[index])

        def each(step, carry):
            push(
                every.at[half], every.at[half + step], far_s.at[index], spread_r.at[index],
                near_peer(step),
            )
            return carry

        lax.fori_loop(1, half, each, 0)

    def await_far(every, index):
        await_bytes(every.at[pl.ds(1, half - 1)], far_r.at[index])
        await_bytes(every.at[pl.ds(half + 1, half - 1)], spread_r.at[index])

    share_near(near_image, 0)

    tile = up_ref.shape[2] // 4

    def turn(index, carry):
        @pl.when(index + ahead < experts)
        def _():
            dispatch(index + ahead, 0)

        @pl.when((index > 0) & (index < experts))
        def _():
            at = index
            await_bytes(rows.at[at, 0], to_expert_r.at[at])
            push(rows.at[at, 0], rows.at[at, 1], fx_s, fx_r.at[at], cross)

        @pl.when(index == 1)
        def _():
            share_far(near_image, all_image, 0)

        @pl.when(index == 3)
        def _():
            load_up.wait()
            load_down.wait()
            await_bytes(up_ref.at[1], core_r.at[0])
            await_bytes(down_ref.at[1], core_r.at[1])

        @pl.when((index >= 3) & (index < experts + 3) & (index % 2 == 1))
        def _():
            at = index - 3
            both = pl.ds(at, 2)
            for later in range(2):
                await_bytes(rows.at[at + later, 1], fx_r.at[at + later])
            block = join(rows[both], 4 * slots)
            term = None
            for side in range(2):
                parts = [
                    gelu(dot(block, up_ref[side, :, low:low + tile])).astype(BF16)
                    for low in range(0, 4 * tile, tile)
                ]
                product = dot_nt(jnp.concatenate(parts, axis=1), down_ref[side])
                term = product if term is None else term + product
            term = part(term, (2, 2))
            own[both] = term[:, 0]
            sum_send[both] = term[:, 1].astype(BF16)
            for later in range(2):
                push(
                    sum_send.at[at + later], sum_in.at[at + later], sum_s, sum_r.at[at + later],
                    cross,
                )

        @pl.when(index == 3)
        def _():
            spread_far(all_image, 0)

        @pl.when(index >= 5)
        def _():
            at = index - 5
            await_bytes(sum_in.at[at], sum_r.at[at])
            result = own[at] + sum_in[at].astype(F32)

            @pl.when(at == 0)
            def _():
                back_in[0] = result.astype(BF16)

            @pl.when(at > 0)
            def _():
                back_send[at] = result.astype(BF16)
                push(back_send.at[at], back_in.at[at], back_s, back_r, expert_peer(at))

        return carry

    lax.fori_loop(0, experts + 5, turn, 0)

    await_bytes(back_in.at[pl.ds(1, experts - 1)], back_r)
    returned = join(back_in[...], experts * slots)
    picked = dot(gate_high[...], returned) + dot(gate_low[...], returned)
    final = layer_norm(tokens_ref[...].astype(F32) + picked) * gain_ref[...]
    starts = jnp.zeros((2 * group, 1), jnp.int32)
    ends = jnp.zeros((2 * group, 1), jnp.int32)
    reached = 0
    for index in range(captions):
        starts = jnp.where(caption == index, reached, starts)
        reached = reached + lengths_ref[0, index]
        ends = jnp.where(caption == index, reached, ends)
    spot = lax.broadcasted_iota(jnp.int32, (2 * group, tokens), 1)
    members = ((spot >= starts) & (spot < ends)).astype(F32).astype(BF16)
    high, low = halves(final)
    pooled = (dot(members, high) + dot(members, low)) / jnp.maximum(ends - starts, 1).astype(F32)
    embed = root_norm(pooled)
    out_ref[0] = embed[group:group + captions]
    direction = embed / math.sqrt(width)
    near_text[0] = direction[:group].astype(BF16)
    own_text[...] = direction[group:].astype(BF16)
    share_near(near_text, 1)
    share_far(near_text, all_text, 1)

    others = pl.ds(1, experts - 1)
    spread_far(all_text, 1)
    await_far(all_image, 0)
    images_all = all_image[...].reshape(experts * group, width)
    offset = g * captions
    out_ref[1] = slope(own_text[...], images_all, offset)[:captions]
    await_far(all_text, 1)
    texts_all = all_text[...].reshape(experts * group, width)
    out_ref[2] = slope(own_image[...], texts_all, offset)[:captions]

    await_bytes(send.at[others], to_expert_s)
    await_bytes(send, fx_s)
    await_bytes(up_ref.at[1], core_s.at[0])
    await_bytes(down_ref.at[1], core_s.at[1])
    await_bytes(sum_send, sum_s)
    await_bytes(back_send.at[others], back_s)
    for index, (near, every) in enumerate(((near_image, all_image), (near_text, all_text))):
        await_bytes(near.at[pl.ds(1, grids - 1)], near_s.at[index])
        await_bytes(every.at[others], far_s.at[index])


def on_device(
    tokens, routes, route_gates, caption_lengths, image_embed, final_gain, up_weight, down_weight
):
    count, width = tokens.shape
    experts, grids = lax.axis_size("expert"), lax.axis_size("grid")
    slots = 4 * count // experts
    captions = caption_lengths.shape[1]
    group = grids * captions
    inner = up_weight.shape[2]
    dma = pltpu.SemaphoreType.DMA
    whole = pl.BlockSpec(memory_space=pltpu.VMEM)
    far = pl.BlockSpec(memory_space=pl.ANY)
    out = jax.ShapeDtypeStruct((3, captions, width), F32)
    scratch = [
        pltpu.VMEM((2, width, inner), BF16),
        pltpu.VMEM((2, width, inner), BF16),
        pltpu.VMEM((experts, slots, width), BF16),
        pltpu.VMEM((count, experts * slots), BF16),
        pltpu.VMEM((count, experts * slots), BF16),
        pltpu.VMEM((experts, 2, slots, width), BF16),
        pltpu.VMEM((experts, slots, width), F32),
    ] + [pltpu.VMEM((experts, slots, width), BF16)] * 4 + [
        pltpu.VMEM((group, width), BF16),
        pltpu.VMEM((grids, group, width), BF16),
        pltpu.VMEM((experts, group, width), BF16),
    ] * 2 + [
        dma((2,)),
        dma, dma((experts,)),
        dma, dma((experts,)),
        dma((2,)), dma((2,)),
        dma, dma((experts,)),
        dma, dma,
        dma((2,)), dma((2,)), dma((2,)), dma((2,)), dma((2,)), dma((2,)),
    ]
    rows = experts * slots * grids
    result = pl.pallas_call(
        functools.partial(kernel, experts, grids, slots, captions),
        out_shape=out,
        in_specs=[pl.BlockSpec(memory_space=pltpu.SMEM)] + [whole] * 5 + [far] * 2,
        out_specs=whole,
        scratch_shapes=scratch,
        cost_estimate=pl.CostEstimate(
            flops=4 * rows * width * inner, bytes_accessed=4 * width * inner,
            transcendentals=rows * inner,
        ),
        compiler_params=pltpu.CompilerParams(
            collective_id=0, has_side_effects=True, vmem_limit_bytes=56 * 1024 * 1024
        ),
    )(
        caption_lengths, tokens, routes.T, route_gates.T, image_embed, final_gain[None, :],
        up_weight[0], down_weight[0],
    )
    return result[0], result[1], result[2]


def solution(mesh):
    split = P(("expert", "grid"), None)
    return jax.shard_map(
        on_device,
        mesh=mesh,
        in_specs=(split,) * 5 + (P(), P("expert", None, "grid"), P("expert", None, "grid")),
        out_specs=(split,) * 3,
        check_vma=False,
    )
```

```python
import functools
import math

import jax
import jax.numpy as jnp
from jax import lax
from jax.experimental import pallas as pl
from jax.experimental.pallas import tpu as pltpu
from jax.sharding import PartitionSpec as P

EPSILON = 1e-06
SIMILARITY_HEAT = 10.0
MESH = pl.DeviceIdType.MESH
BF16 = jnp.bfloat16
F32 = jnp.float32


def layer_norm(values):
    centred = values - jnp.mean(values, axis=-1, keepdims=True)
    return centred * lax.rsqrt(jnp.mean(centred * centred, axis=-1, keepdims=True) + EPSILON)


def root_norm(values):
    return values * lax.rsqrt(jnp.mean(values * values, axis=-1, keepdims=True) + EPSILON)


def flip(one, other, count):
    total, bit = 0, 1
    while bit < count:
        total = total + bit * (((one // bit) + (other // bit)) % 2)
        bit *= 2
    return total


def halves(values):
    high = values.astype(BF16)
    return high, (values - high.astype(F32)).astype(BF16)


def dot(left, right):
    return jnp.dot(left, right, preferred_element_type=F32)


def dot_nt(left, right):
    return lax.dot_general(left, right, (((1,), (1,)), ((), ())), preferred_element_type=F32)


def join(values, rows):
    width = values.shape[-1]
    if values.shape[-2] % 16 == 0:
        return values.reshape(rows, width)
    return values.astype(F32).reshape(rows, width).astype(values.dtype)


def part(values, lead):
    return values.reshape(lead + (values.shape[0] // math.prod(lead), values.shape[-1]))


def gelu(values):
    size = jnp.abs(values)
    t = 1.0 / (1.0 + (0.3275911 * math.sqrt(0.5)) * size)
    series = 0.5 * 1.061405429
    for term in (-1.453152027, 1.421413741, -0.284496736, 0.254829592):
        series = series * t + 0.5 * term
    tail = series * t * jnp.exp(values * values * -0.5)
    return jnp.maximum(values, 0.0) - size * tail


def slope(own, every, offset):
    logits = SIMILARITY_HEAT * dot_nt(own, every)
    row = lax.broadcasted_iota(jnp.int32, logits.shape, 0)
    column = lax.broadcasted_iota(jnp.int32, logits.shape, 1)
    signs = jnp.where(column == row + offset, 1.0, -1.0).astype(F32)
    coeff = -signs * jax.nn.sigmoid(-signs * logits)
    high, low = halves(coeff)
    return SIMILARITY_HEAT * (dot(high, every) + dot(low, every))


def kernel(
    experts, grids, slots, captions,
    lengths_ref, tokens_ref, routes_ref, gates_ref, image_ref, gain_ref, up_hbm, down_hbm,
    out_ref,
    up_ref, down_ref, down_turned, send, gate_high, gate_low, rows, own, part_send, part_in, sum_send, sum_in,
    back_send, back_in, own_image, near_image, all_image, own_text, near_text, all_text,
    weight_sem, to_expert_s, to_expert_r, fx_s, fx_r, fc_s, fc_r, part_s, part_r, sum_s, sum_r,
    back_s, back_r, near_s, near_r, far_s, far_r, across_r, spread_r,
):
    e = lax.axis_index("expert")
    g = lax.axis_index("grid")
    core = (e, g + 1 - 2 * (g % 2))
    cross = (e, (g + grids // 2) % grids)
    tokens, width = tokens_ref.shape
    group = grids * captions

    half = experts // 2

    def order(position):
        turned = position + experts - 1
        turn_of = turned % experts
        pair, odd = turn_of // 2 + 1, turn_of % 2
        return (turned // experts) * ((1 - odd) * pair + odd * (half + pair % half))

    opposite = ((e + half) % experts, g)

    def near_peer(step):
        return (flip(e, step, experts), g)

    def expert_peer(step):
        return (flip(e, order(step), experts), g)

    def push(source, target, send_sem, recv_sem, device):
        pltpu.make_async_remote_copy(
            src_ref=source, dst_ref=target, send_sem=send_sem, recv_sem=recv_sem,
            device_id=device, device_id_type=MESH,
        ).start()

    def await_bytes(ref, sem):
        pltpu.make_async_copy(ref, ref, sem).wait()

    barrier = pltpu.get_barrier_semaphore()

    def greet(step, carry):
        pl.semaphore_signal(barrier, inc=1, device_id=expert_peer(step), device_id_type=MESH)
        return carry

    lax.fori_loop(1, experts, greet, 0)
    for hop in range(1, grids):
        pl.semaphore_signal(barrier, inc=1, device_id=(e, (g + hop) % grids), device_id_type=MESH)
    load_up = pltpu.make_async_copy(up_hbm, up_ref, weight_sem.at[0])
    load_up.start()
    load_down = pltpu.make_async_copy(down_hbm, down_ref, weight_sem.at[1])
    load_down.start()

    normed = layer_norm(tokens_ref[...].astype(F32)).astype(BF16)
    routes = routes_ref[...]
    first, second = routes[0:1, :], routes[1:2, :]
    ids = lax.broadcasted_iota(jnp.int32, (max(experts, 8), tokens), 0)
    named = ((ids == first) | (ids == second)).astype(F32).astype(BF16)
    before = lax.broadcasted_iota(jnp.int32, (tokens, tokens), 0)
    after = lax.broadcasted_iota(jnp.int32, (tokens, tokens), 1)
    ranks = dot(named, (before < after).astype(F32).astype(BF16))
    spots = lax.broadcasted_iota(jnp.int32, (experts * slots, tokens), 0)
    hits = []
    for chosen in (first, second):
        rank = jnp.sum(jnp.where(ids == chosen, ranks, 0.0), axis=0, keepdims=True)
        far = flip(chosen, e, experts)
        spot_of = jnp.where(far > half, 2 * (far - half), jnp.maximum(2 * far - 1, 0))
        hits.append(spots == spot_of * slots + rank.astype(jnp.int32))
    taken = (hits[0] | hits[1]).astype(F32).astype(BF16)
    blocks = part(dot(taken, normed), (experts,)).astype(BF16)
    send[...] = blocks
    rows[0, 0] = blocks[0]
    pl.semaphore_wait(barrier, experts + grids - 2)

    def dispatch(step, carry):
        push(send.at[step], rows.at[step, 0], to_expert_s, to_expert_r.at[step], expert_peer(step))
        return carry

    ahead = experts
    lax.fori_loop(1, ahead, dispatch, 0)
    push(rows.at[0, 0], rows.at[0, 1], fx_s, fx_r.at[0], cross)
    push(rows.at[0, 0], rows.at[0, 2], fc_s, fc_r.at[0], core)
    weights = jnp.where(hits[0], gates_ref[0:1, :], 0.0) + jnp.where(hits[1], gates_ref[1:2, :], 0.0)
    high, low = halves(weights.T)
    gate_high[...] = high
    gate_low[...] = low

    line = lax.broadcasted_iota(jnp.int32, (2 * group, 1), 0)
    caption = jnp.where(line < group, line - g * captions, line - group)
    images = root_norm(image_ref[...].astype(F32)) / math.sqrt(width)
    spread = jnp.zeros((2 * group, width), F32)
    for index in range(captions):
        spread = jnp.where(caption == index, images[index:index + 1, :], spread)
    near_image[0] = spread[:group].astype(BF16)
    own_image[...] = spread[group:].astype(BF16)

    def share_near(near, index):
        for hop in range(1, grids):
            push(near.at[0], near.at[hop], near_s.at[index], near_r.at[index], (e, (g + hop) % grids))

    def share_far(near, every, index):
        await_bytes(near.at[pl.ds(1, grids - 1)], near_r.at[index])
        total = near[0].astype(F32)
        for hop in range(1, grids):
            total = total + near[hop].astype(F32)
        every[0] = total.astype(BF16)

        push(every.at[0], every.at[half], far_s.at[index], across_r.at[index], opposite)

        def each(step, carry):
            push(every.at[0], every.at[step], far_s.at[index], far_r.at[index], near_peer(step))
            return carry

        lax.fori_loop(1, half, each, 0)

    def spread_far(every, index):
        await_bytes(every.at[half], across_r.at[index])

        def each(step, carry):
            push(
                every.at[half], every.at[half + step], far_s.at[index], spread_r.at[index],
                near_peer(step),
            )
            return carry

        lax.fori_loop(1, half, each, 0)

    def await_far(every, index):
        await_bytes(every.at[pl.ds(1, half - 1)], far_r.at[index])
        await_bytes(every.at[pl.ds(half + 1, half - 1)], spread_r.at[index])

    share_near(near_image, 0)

    tile = up_ref.shape[1] // 4

    def turn(index, carry):
        @pl.when(index + ahead < experts)
        def _():
            dispatch(index + ahead, 0)

        @pl.when((index > 0) & (index < experts))
        def _():
            at = index
            await_bytes(rows.at[at, 0], to_expert_r.at[at])
            push(rows.at[at, 0], rows.at[at, 1], fx_s, fx_r.at[at], cross)
            push(rows.at[at, 0], rows.at[at, 2], fc_s, fc_r.at[at], core)

        @pl.when((index >= 2) & (index < experts + 2))
        def _():
            at = index - 2
            await_bytes(rows.at[at, 1], fx_r.at[at])
            push(rows.at[at, 1], rows.at[at, 3], fc_s, fc_r.at[at], core)

        @pl.when(index == 1)
        def _():
            share_far(near_image, all_image, 0)
            load_up.wait()
            load_down.wait()
            for low in range(0, 4 * tile, tile):
                down_turned[low:low + tile] = down_ref[:, low:low + tile].T

        @pl.when((index >= 3) & (index < experts + 3))
        def _():
            at = index - 3
            await_bytes(rows.at[at, pl.ds(2, 2)], fc_r.at[at])
            block = join(rows[at], grids * slots)
            parts = [
                gelu(dot(block, up_ref[:, low:low + tile])).astype(BF16)
                for low in range(0, 4 * tile, tile)
            ]
            term = part(dot(jnp.concatenate(parts, axis=1), down_turned[...]), (grids,))
            own[at] = term[:2]
            part_send[at] = term[2:].astype(BF16)
            push(part_send.at[at], part_in.at[at], part_s, part_r.at[at], core)

        @pl.when(index == 3)
        def _():
            spread_far(all_image, 0)

        @pl.when((index >= 4) & (index < experts + 4))
        def _():
            at = index - 4
            await_bytes(part_in.at[at], part_r.at[at])
            sum_send[at] = (own[at, 1] + part_in[at, 1].astype(F32)).astype(BF16)
            push(sum_send.at[at], sum_in.at[at], sum_s, sum_r.at[at], cross)

        @pl.when(index >= 6)
        def _():
            at = index - 6
            await_bytes(sum_in.at[at], sum_r.at[at])
            result = own[at, 0] + part_in[at, 0].astype(F32) + sum_in[at].astype(F32)

            @pl.when(at == 0)
            def _():
                back_in[0] = result.astype(BF16)

            @pl.when(at > 0)
            def _():
                back_send[at] = result.astype(BF16)
                push(back_send.at[at], back_in.at[at], back_s, back_r, expert_peer(at))

        return carry

    lax.fori_loop(0, experts + 6, turn, 0)

    await_bytes(back_in.at[pl.ds(1, experts - 1)], back_r)
    returned = join(back_in[...], experts * slots)
    picked = dot(gate_high[...], returned) + dot(gate_low[...], returned)
    final = layer_norm(tokens_ref[...].astype(F32) + picked) * gain_ref[...]
    starts = jnp.zeros((2 * group, 1), jnp.int32)
    ends = jnp.zeros((2 * group, 1), jnp.int32)
    reached = 0
    for index in range(captions):
        starts = jnp.where(caption == index, reached, starts)
        reached = reached + lengths_ref[0, index]
        ends = jnp.where(caption == index, reached, ends)
    spot = lax.broadcasted_iota(jnp.int32, (2 * group, tokens), 1)
    members = ((spot >= starts) & (spot < ends)).astype(F32).astype(BF16)
    high, low = halves(final)
    pooled = (dot(members, high) + dot(members, low)) / jnp.maximum(ends - starts, 1).astype(F32)
    embed = root_norm(pooled)
    out_ref[0] = embed[group:group + captions]
    direction = embed / math.sqrt(width)
    near_text[0] = direction[:group].astype(BF16)
    own_text[...] = direction[group:].astype(BF16)
    share_near(near_text, 1)
    share_far(near_text, all_text, 1)

    others = pl.ds(1, experts - 1)
    spread_far(all_text, 1)
    await_far(all_image, 0)
    images_all = all_image[...].reshape(experts * group, width)
    offset = g * captions
    out_ref[1] = slope(own_text[...], images_all, offset)[:captions]
    await_far(all_text, 1)
    texts_all = all_text[...].reshape(experts * group, width)
    out_ref[2] = slope(own_image[...], texts_all, offset)[:captions]

    await_bytes(send.at[others], to_expert_s)
    await_bytes(send, fx_s)
    await_bytes(part_send, fc_s)
    await_bytes(part_send, part_s)
    await_bytes(sum_send, sum_s)
    await_bytes(back_send.at[others], back_s)
    for index, (near, every) in enumerate(((near_image, all_image), (near_text, all_text))):
        await_bytes(near.at[pl.ds(1, grids - 1)], near_s.at[index])
        await_bytes(every.at[others], far_s.at[index])


def on_device(
    tokens, routes, route_gates, caption_lengths, image_embed, final_gain, up_weight, down_weight
):
    count, width = tokens.shape
    experts, grids = lax.axis_size("expert"), lax.axis_size("grid")
    slots = 4 * count // experts
    captions = caption_lengths.shape[1]
    group = grids * captions
    inner = up_weight.shape[2]
    dma = pltpu.SemaphoreType.DMA
    whole = pl.BlockSpec(memory_space=pltpu.VMEM)
    far = pl.BlockSpec(memory_space=pl.ANY)
    out = jax.ShapeDtypeStruct((3, captions, width), F32)
    scratch = [
        pltpu.VMEM((width, inner), BF16),
        pltpu.VMEM((width, inner), BF16),
        pltpu.VMEM((inner, width), BF16),
        pltpu.VMEM((experts, slots, width), BF16),
        pltpu.VMEM((count, experts * slots), BF16),
        pltpu.VMEM((count, experts * slots), BF16),
        pltpu.VMEM((experts, grids, slots, width), BF16),
        pltpu.VMEM((experts, 2, slots, width), F32),
        pltpu.VMEM((experts, 2, slots, width), BF16),
        pltpu.VMEM((experts, 2, slots, width), BF16),
    ] + [pltpu.VMEM((experts, slots, width), BF16)] * 4 + [
        pltpu.VMEM((group, width), BF16),
        pltpu.VMEM((grids, group, width), BF16),
        pltpu.VMEM((experts, group, width), BF16),
    ] * 2 + [
        dma((2,)),
        dma, dma((experts,)),
        dma, dma((experts,)),
        dma, dma((experts,)),
        dma, dma((experts,)),
        dma, dma((experts,)),
        dma, dma,
        dma((2,)), dma((2,)), dma((2,)), dma((2,)), dma((2,)), dma((2,)),
    ]
    rows = experts * slots * grids
    result = pl.pallas_call(
        functools.partial(kernel, experts, grids, slots, captions),
        out_shape=out,
        in_specs=[pl.BlockSpec(memory_space=pltpu.SMEM)] + [whole] * 5 + [far] * 2,
        out_specs=whole,
        scratch_shapes=scratch,
        cost_estimate=pl.CostEstimate(
            flops=4 * rows * width * inner, bytes_accessed=4 * width * inner,
            transcendentals=rows * inner,
        ),
        compiler_params=pltpu.CompilerParams(
            collective_id=0, has_side_effects=True, vmem_limit_bytes=56 * 1024 * 1024
        ),
    )(
        caption_lengths, tokens, routes.T, route_gates.T, image_embed, final_gain[None, :],
        up_weight[0], down_weight[0],
    )
    return result[0], result[1], result[2]


def solution(mesh):
    split = P(("expert", "grid"), None)
    return jax.shard_map(
        on_device,
        mesh=mesh,
        in_specs=(split,) * 5 + (P(), P("expert", None, "grid"), P("expert", None, "grid")),
        out_specs=(split,) * 3,
        check_vma=False,
    )
```
